256 devices in a mesh: wide: 64 (over y_hi, x, z), narrow: 4 (over y_lo, core).
Axes of the slice: x: 4, y: 4 (y_hi: 2, y_lo: 2; y = y_hi * 2 + y_lo), z: 8, core: 2. Of those that a mesh axis runs over, the one named last changes fastest.
Arguments:
- src_emb: float32 [65536, 400], P(('wide', 'narrow')), may hold values from -1.5 to 1.5
- src_state: float32 [65536], P(('wide', 'narrow')), may hold values from 0.0001 to 0.01
- dst_emb: float32 [65536, 400], P('wide'), may hold values from -1.5 to 1.5
- dst_state: float32 [65536], P('wide'), may hold values from 0.0001 to 0.01
- relations: bfloat16 [7424, 400], replicated, may hold values from -3 to 3
- src_index: int32 [256, 2, 256], P(('wide', 'narrow')), may hold values from 0 to 255
- dst_index: int32 [256, 2, 256], P(('wide', 'narrow')), may hold values from 0 to 1023
- rel_index: int32 [256, 2, 256], P(('wide', 'narrow')), may hold values from 0 to 7423
- neg_index: int32 [64, 2, 2048], P('wide'), may hold values from 0 to 1023
Outputs:
- src_out: float32 [65536, 400], P(('wide', 'narrow'))
- dst_out: float32 [65536, 400], P('wide')
The draws below stay inside these ranges and needn't reach their ends.
All inputs are finite; a program needn't handle non-finite values.
Results may differ from the reference program's by a relative error of at most 0.0029.
Values may be sent and summed in bfloat16 or wider, within the bound.
No kernel may reach another device: no remote copies, remote signals or barrier semaphores. Data moves between devices by JAX's collectives and lax.ppermute only.
A program may use at most 128 MiB of HBM per device.

```python
import math
import jax
import jax.numpy as jnp
import numpy as np
from jax import lax

D = 400
REL = 7424
NEG = 2048
STEPS = 2
SRC_DEV = 256
DST_ROWS = 1024
EDGE_DEV = 256
PARTITIONS = 64
GROUPS = 256
SRC_ALL = 65536
DST_ALL = 65536
N_WIDE = 64
N_NARROW = 4


def touch_ends(result, rng, smallest, largest):
    spot = [jax.random.randint(jax.random.fold_in(rng, axis), (), 0, length) for axis, length in enumerate(result.shape)]
    widest = result.shape.index(max(result.shape))
    next_to = spot[:widest] + [(spot[widest] + 1) % result.shape[widest]] + spot[widest + 1:]
    return result.at[tuple(spot)].set(smallest).at[tuple(next_to)].set(largest)


def shard_levels(key, dims, pieces, smallest, top_value):
    loudness = 1.0
    for axis_at, parts in pieces:
        heights = jax.random.uniform(jax.random.fold_in(jax.random.fold_in(key, 6), axis_at), (parts,), jnp.float32, smallest / len(pieces), top_value / len(pieces))
        loudness = loudness * jnp.repeat(jnp.exp(heights), dims[axis_at] // parts).reshape((-1,) + (1,) * (len(dims) - 1 - axis_at))
    return loudness


def rank_table(count, slope):
    weights = [(1 << 20) // math.isqrt(standing ** slope) + 1 for standing in range(1, count + 1)]
    scale = 1 + sum(weights) // (1 << 30)
    return np.cumsum(np.array([max(1, weight // scale) for weight in weights]))


def ranked(rng, dims, count, lean):
    table = rank_table(count, lean)
    ticket = jax.random.randint(jax.random.fold_in(rng, 1), dims, 0, int(table[count - 1]))
    rank = jnp.searchsorted(jnp.asarray(table, jnp.int32), ticket, side="right")
    return jax.random.permutation(jax.random.fold_in(rng, 2), count)[rank].astype(jnp.int32)


def gaussian(own_key, dims, spread, most, shards=(), held_as=jnp.bfloat16):
    drawn = spread * jax.random.normal(own_key, dims, jnp.float32)
    if shards:
        drawn = drawn * shard_levels(own_key, dims, shards, -0.22, 0.18)
    return jnp.clip(drawn, -most, most).astype(held_as)


def setup_inputs(seed: int = 0) -> dict:
    key_list = jax.random.split(jax.random.key(seed), 10)
    src_emb = gaussian(key_list[0], (SRC_ALL, D), 0.5, 1.5, ((0, 256),), jnp.float32)
    src_state = jnp.clip(jnp.exp(math.log(0.01) - 4.6051702 * jax.random.uniform(key_list[1], (SRC_ALL,), jnp.float32) ** shard_levels(key_list[1], (SRC_ALL,), ((0, 256),), -0.2, 0.2)), 0.0001, 0.01)
    dst_emb = gaussian(key_list[2], (DST_ALL, D), 0.5, 1.5, ((0, 64),), jnp.float32)
    dst_state = jnp.clip(jnp.exp(math.log(0.01) - 4.6051702 * jax.random.uniform(key_list[3], (DST_ALL,), jnp.float32) ** shard_levels(key_list[3], (DST_ALL,), ((0, 64),), -0.2, 0.2)), 0.0001, 0.01)
    relations = gaussian(key_list[4], (REL, D), 1.0, 3.0)
    src_index = touch_ends(jax.random.randint(key_list[5], (GROUPS, STEPS, EDGE_DEV), 0, SRC_DEV), jax.random.fold_in(key_list[5], 1), 0, SRC_DEV - 1).astype(jnp.int32)
    dst_index = touch_ends(jax.random.randint(key_list[6], (GROUPS, STEPS, EDGE_DEV), 0, DST_ROWS), jax.random.fold_in(key_list[6], 1), 0, DST_ROWS - 1).astype(jnp.int32)
    rel_index = touch_ends(ranked(key_list[7], (GROUPS, STEPS, EDGE_DEV), REL, 2), jax.random.fold_in(key_list[7], 3), 0, REL - 1).astype(jnp.int32)
    neg_index = touch_ends(jax.random.randint(key_list[8], (PARTITIONS, STEPS, NEG), 0, DST_ROWS), jax.random.fold_in(key_list[8], 1), 0, DST_ROWS - 1).astype(jnp.int32)
    return {"src_emb": src_emb, "src_state": src_state, "dst_emb": dst_emb, "dst_state": dst_state, "relations": relations, "src_index": src_index, "dst_index": dst_index, "rel_index": rel_index, "neg_index": neg_index}


LEARNING_RATE = 0.1

def bucket_grads(src_rows, relations, block_bf, src_pick, dst_pick, rel_pick, neg_pick):
    rel_rows = relations[rel_pick].astype(jnp.float32)
    query_bf = (src_rows[src_pick] * rel_rows).astype(jnp.bfloat16)
    target = block_bf[dst_pick]
    positive = lax.optimization_barrier(jnp.sum(query_bf.astype(jnp.float32) * target.astype(jnp.float32), axis=-1))
    neg_rows = block_bf[neg_pick]
    scores = lax.dot_general(query_bf, neg_rows, (((1,), (1,)), ((), ())), preferred_element_type=jnp.float32)
    weights = (jax.nn.sigmoid(scores) / neg_rows.shape[0]).astype(jnp.bfloat16)
    pull_grad = -jax.nn.sigmoid(-positive)
    query_grad = pull_grad[:, None] * target.astype(jnp.float32) + jnp.dot(weights, neg_rows, preferred_element_type=jnp.float32)
    src_grad = jnp.zeros(src_rows.shape, jnp.float32).at[src_pick].add(query_grad * rel_rows)
    neg_grad = lax.dot_general(weights, query_bf, (((0,), (0,)), ((), ())), preferred_element_type=jnp.float32)
    dst_grad = jnp.zeros(block_bf.shape, jnp.float32).at[dst_pick].add(pull_grad[:, None] * query_bf.astype(jnp.float32))
    dst_grad = dst_grad.at[neg_pick].add(neg_grad)
    return (src_grad, dst_grad)

def adagrad(embedding, accum_state, gradient):
    accum_state = accum_state + lax.optimization_barrier(jnp.mean(gradient * gradient, axis=-1))
    return (embedding - LEARNING_RATE * gradient / jnp.sqrt(accum_state)[:, None], accum_state)

def reference(src_emb, src_state, dst_emb, dst_state, relations, src_index, dst_index, rel_index, neg_index):
    source = src_emb.reshape(N_WIDE, N_NARROW * SRC_DEV, D)
    source_state = src_state.reshape(N_WIDE, N_NARROW * SRC_DEV)
    offsets = (jnp.arange(N_NARROW, dtype=jnp.int32) * SRC_DEV)[:, None].astype(jnp.int32)
    for bucket in range(STEPS):
        dest_bf = dst_emb.astype(jnp.bfloat16).reshape(N_WIDE, DST_ROWS, D)
        blocks = jnp.roll(dest_bf, bucket + 1, axis=0)
        src_pick = (src_index[:, bucket].reshape(N_WIDE, N_NARROW, EDGE_DEV) + offsets).reshape(N_WIDE, N_NARROW * EDGE_DEV)
        dst_pick = dst_index[:, bucket].reshape(N_WIDE, N_NARROW * EDGE_DEV)
        rel_pick = rel_index[:, bucket].reshape(N_WIDE, N_NARROW * EDGE_DEV)
        neg_pick = neg_index[:, bucket]

        def per_partition(operands):
            return bucket_grads(operands[0], relations, operands[1], operands[2], operands[3], operands[4], operands[5])
        src_grad, dst_grad = lax.map(per_partition, (source, blocks, src_pick, dst_pick, rel_pick, neg_pick))
        dst_grad = jnp.roll(dst_grad, -(bucket + 1), axis=0)
        flat_source, flat_state = adagrad(source.reshape(-1, D), source_state.reshape(-1), src_grad.reshape(-1, D))
        source = flat_source.reshape(N_WIDE, N_NARROW * SRC_DEV, D)
        source_state = flat_state.reshape(N_WIDE, N_NARROW * SRC_DEV)
        dst_emb, dst_state = adagrad(dst_emb, dst_state, dst_grad.reshape(-1, D))
    return (source.reshape(-1, D), dst_emb)
```

```python
import functools

import jax
import jax.numpy as jnp
from jax import lax
from jax.experimental import pallas as pl
from jax.experimental.pallas import tpu as pltpu
from jax.sharding import PartitionSpec as P

LEARNING_RATE = 0.1
BF = jnp.bfloat16
F32 = jnp.float32
I32 = jnp.int32
META = 16
FINE = 32
LANES = 128


def dot(a, b):
    return lax.dot_general(a, b, (((1,), (0,)), ((), ())), preferred_element_type=F32)


def dot_nt(a, b):
    return lax.dot_general(a, b, (((1,), (1,)), ((), ())), preferred_element_type=F32)


def core():
    return lax.rem(lax.axis_index("narrow"), 2)


def iota(shape, dim):
    return lax.broadcasted_iota(I32, shape, dim)


def one_hot(rows, index):
    return (iota((rows, index.shape[1]), 0) == index).astype(F32).astype(BF)


def eye(n):
    return (iota((n, n), 0) == iota((n, n), 1)).astype(F32).astype(BF)


def two_rows(first, second, width):
    at = iota((META, width), 0)
    return jnp.where(at == 0, first, jnp.where(at == 1, second, 0.0)).astype(BF)


def index_rows(index):
    fine = lax.rem(index, FINE)
    coarse = lax.div(index, FINE)
    return two_rows(coarse.astype(F32), fine.astype(F32), index.shape[1])


def split(value):
    high = value.astype(BF)
    return high, (value - high.astype(F32)).astype(BF)


def picked(value, hot):
    high, low = split(value)
    return dot(high, hot) + dot(low, hot)


def summed(value, hot):
    high, low = split(value)
    return dot_nt(high, hot) + dot_nt(low, hot)


def coefficients(scores, count, is_target, negatives):
    tanh = jnp.tanh(0.5 * scores)
    scale = count * (0.5 / negatives)
    pull = jnp.where(is_target, 0.5 * tanh - 0.5, 0.0)
    return (scale * tanh + scale + pull).astype(BF)


def step_size(state, gradient):
    state = state + jnp.mean(gradient * gradient, axis=0, keepdims=True)
    return state, LEARNING_RATE / jnp.sqrt(state)


def cast_kernel(emb_ref, state_ref, out_ref, held, sem):
    depth, half = held.shape
    columns = pl.ds(pl.multiple_of(core() * half, half), half)
    copy = pltpu.make_async_copy(emb_ref.at[:, columns], held, sem)
    copy.start()
    state = state_ref[:, columns]
    high = state.astype(BF).astype(F32)
    out_ref[depth:, :] = two_rows(high, state - high, half)
    copy.wait()
    out_ref[:depth, :] = held[...].astype(BF)


def count_grid(index, blocks):
    return one_hot(blocks, lax.div(index, LANES)), one_hot(LANES, lax.rem(index, LANES))


def prep_kernel(
    chunks, rows, rel_ref, src_ref, src_index, dst_index, rel_index, neg_index,
    q_ref, qt_ref, at_ref, rel0_ref, rel1_ref, count_ref, column_ref, held, sems,
):
    depth, edges = src_ref.shape
    copies = []
    start = 0
    for i, size in enumerate(chunks):
        part = pl.ds(start, size)
        copies.append(pltpu.make_async_copy(rel_ref.at[:, part], held.at[:, part], sems.at[i]))
        copies[-1].start()
        start += size

    flip = core() * (rows // 2)
    coarse, fine = count_grid(neg_index[0:1, :] ^ flip, rows // LANES)
    counts = dot_nt(coarse, fine)
    for i in range(rows // LANES):
        count_ref[:, i * LANES : (i + 1) * LANES] = counts[i : i + 1, :]
    column_ref[...] = dot_nt(fine, coarse)

    src_rows = picked(src_ref[...], one_hot(edges, src_index[0:1, :]))
    which = jnp.concatenate([rel_index[0:1, :], rel_index[1:2, :]], axis=1)
    block = lax.div(which, LANES)
    within = one_hot(LANES, lax.rem(which, LANES))
    found = jnp.zeros((depth, 2 * edges), F32)
    start = 0
    for copy, size in zip(copies, chunks):
        hot = jnp.concatenate(
            [
                within * (block == start // LANES + i).astype(F32).astype(BF)
                for i in range(size // LANES)
            ],
            axis=0,
        )
        copy.wait()
        found = found + dot(held[:, start : start + size], hot)
        start += size
    rel0_ref[...] = found[:, :edges].astype(BF)
    rel1_ref[...] = found[:, edges:].astype(BF)
    query = (src_rows * found[:, :edges]).astype(BF)
    meta = index_rows(dst_index[0:1, :])
    q_ref[:depth, :] = query
    q_ref[depth:, :] = meta
    turn = eye(edges)
    qt_ref[...] = dot_nt(turn, query).astype(BF)
    parts = dot_nt(turn, meta)
    local = (parts[:, 0:1] * FINE + parts[:, 1:2]).astype(I32) ^ flip
    at_ref[...] = jnp.broadcast_to(local, at_ref.shape)


def src0_kernel(
    negatives, own_ref, other_ref, qt_ref, at_ref, count_ref, src_ref, state_ref,
    rel0_ref, rel1_ref, src_index, dst_index, q_ref, src_out, state_out,
):
    depth, edges = src_ref.shape
    half = own_ref.shape[1]
    query_grad = jnp.zeros((depth, edges), F32)
    for i, block_ref in enumerate((own_ref, other_ref)):
        block = block_ref[:depth, :]
        scores = dot(qt_ref[...], block)
        target = iota(scores.shape, 1) + i * half == at_ref[:, 0:1]
        count = count_ref[:, i * half : (i + 1) * half]
        query_grad += dot_nt(block, coefficients(scores, count, target, negatives))
    gradient = summed(
        query_grad * rel0_ref[...].astype(F32), one_hot(edges, src_index[0:1, :])
    )
    state, size = step_size(state_ref[...], gradient)
    src = src_ref[...] - gradient * size
    src_out[...] = src
    state_out[...] = state
    rows = picked(src, one_hot(edges, src_index[1:2, :]))
    q_ref[:depth, :] = (rows * rel1_ref[...].astype(F32)).astype(BF)
    q_ref[depth:, :] = index_rows(dst_index[1:2, :])


def targets(q_ref, depth, flip):
    parts = q_ref[depth:, :].astype(F32)
    return (parts[0:1, :] * FINE + parts[1:2, :]).astype(I32) ^ flip


def row_coefficients(block_t, start, q_ref, column, flip, negatives):
    rows, depth = block_t.shape
    scores = dot(block_t, q_ref[:depth, :])
    target = iota(scores.shape, 0) + start == targets(q_ref, depth, flip)
    first = start // LANES
    count = jnp.concatenate(
        [column[:, first + i : first + i + 1] for i in range(rows // LANES)], axis=0
    )
    return coefficients(scores, count, target, negatives)


def dst_gradient(block_t, start, q_refs, column, flip, negatives):
    rows, depth = block_t.shape
    total = jnp.zeros((depth, rows), F32)
    for q_ref in q_refs:
        weights = row_coefficients(block_t, start, q_ref, column, flip, negatives)
        total += dot_nt(q_ref[:depth, :], weights)
    return total


def dst0_kernel(
    negatives, own_ref, other_ref, qa, qb, qc, qd, column_ref, neg_index,
    block_out, turned_out, delta_out, state_out, column_out,
):
    depth, half = delta_out.shape
    flip = core() * half
    turn = eye(2 * LANES)
    column = column_ref[...]
    for i, block_ref in enumerate((own_ref, other_ref)):
        block = block_ref[:depth, :]
        turned = jnp.concatenate(
            [
                dot_nt(turn, block[:, k : k + 2 * LANES]).astype(BF)
                for k in range(0, half, 2 * LANES)
            ],
            axis=0,
        )
        gradient = dst_gradient(turned, i * half, (qa, qb, qc, qd), column, flip, negatives)
        parts = block_ref[depth:, :].astype(F32)
        state, size = step_size(parts[0:1, :] + parts[1:2, :], gradient)
        delta = gradient * size
        block = (block.astype(F32) - delta).astype(BF)
        block_out[:, i * half : (i + 1) * half] = block
        for k in range(0, half, 2 * LANES):
            turned_out[i * half + k : i * half + k + 2 * LANES, :] = dot_nt(
                turn, block[:, k : k + 2 * LANES]
            ).astype(BF)
        if i == 0:
            delta_out[...] = delta
            state_out[...] = state
    coarse, fine = count_grid(neg_index[...] ^ flip, 2 * half // LANES)
    column_out[...] = dot_nt(fine, coarse)


def dst1_kernel(
    negatives, turned_ref, qa, qb, qc, qd, column_ref, delta_ref, state_ref, delta_out
):
    half = delta_ref.shape[1]
    flip = core() * half
    gradient = dst_gradient(
        turned_ref[:half, :], 0, (qa, qb, qc, qd), column_ref[...], flip, negatives
    )
    _, size = step_size(state_ref[...], gradient)
    delta_out[...] = (delta_ref[...] + gradient * size).astype(BF)


def query1_kernel(negatives, turned_ref, block_ref, q_ref, column_ref, out_ref):
    rows = turned_ref.shape[0]
    weights = row_coefficients(
        turned_ref[...], 0, q_ref, column_ref[...], core() * (rows // 2), negatives
    )
    out_ref[...] = dot(block_ref[...], weights).astype(BF)


def src1_kernel(grad_ref, rel_ref, src_ref, state_ref, src_index, src_out):
    edges = src_ref.shape[1]
    gradient = summed(
        grad_ref[...].astype(F32) * rel_ref[...].astype(F32), one_hot(edges, src_index[1:2, :])
    )
    _, size = step_size(state_ref[...], gradient)
    src_out[...] = src_ref[...] - gradient * size


def final_kernel(emb_ref, own_ref, other_ref, out_ref):
    half = own_ref.shape[1]
    here = core()
    for place, delta_ref in ((here, own_ref), (1 - here, other_ref)):
        columns = pl.ds(pl.multiple_of(place * half, half), half)
        out_ref[:, columns] = emb_ref[:, columns] - delta_ref[...].astype(F32)


def call(kernel, outs, args, name, flops=0, scratch=(), hbm=(), limit=32):
    vmem = pl.BlockSpec(memory_space=pltpu.VMEM)
    anywhere = pl.BlockSpec(memory_space=pl.ANY)
    shapes = [jax.ShapeDtypeStruct(shape, dtype) for shape, dtype in outs]
    size = sum(a.size * a.dtype.itemsize for a in [*args, *shapes])
    result = pl.pallas_call(
        kernel,
        out_shape=shapes,
        in_specs=[anywhere if i in hbm else vmem for i in range(len(args))],
        out_specs=[vmem] * len(shapes),
        scratch_shapes=list(scratch),
        compiler_params=pltpu.CompilerParams(vmem_limit_bytes=limit << 20),
        cost_estimate=pl.CostEstimate(flops=flops, bytes_accessed=size, transcendentals=0),
        name=name,
    )(*args)
    return result[0] if len(shapes) == 1 else result


def body(
    src_emb, src_state, dst_emb, dst_state, relations, src_index, dst_index, rel_index, neg_index
):
    wide, narrow = lax.axis_size("wide"), lax.axis_size("narrow")

    def moved(value, along=0, to=0):
        pairs = [
            (w * narrow + n, ((w + along) % wide) * narrow + (n ^ to))
            for w in range(wide)
            for n in range(narrow)
        ]
        return lax.ppermute(value, ("wide", "narrow"), pairs)

    rows, depth = dst_emb.shape
    edges = src_emb.shape[0]
    half = rows // 2
    relation_count = relations.shape[0]
    src_index, dst_index, rel_index, neg_index = (
        a[0] for a in (src_index, dst_index, rel_index, neg_index)
    )
    negatives = neg_index.shape[1]
    dst, src, rel = dst_emb.T, src_emb.T, relations.T
    tall = depth + META

    payload = call(
        cast_kernel,
        [((tall, half), BF)],
        [dst, dst_state.reshape(1, rows)],
        "cast_block",
        scratch=[pltpu.VMEM((depth, half), F32), pltpu.SemaphoreType.DMA],
        hbm=(0,),
        limit=8,
    )
    own = moved(payload, along=1)
    negs_next = moved(neg_index[1:2, :], along=-1)

    pieces = relation_count // (2 * LANES)
    chunks = [(pieces // 4 + (i < pieces % 4)) * 2 * LANES for i in range(4)]
    chunks[-1] += relation_count - sum(chunks)
    query, query_t, target_at, rel0, rel1, count, column = call(
        functools.partial(prep_kernel, tuple(chunks), rows),
        [
            ((tall, edges), BF),
            ((edges, depth), BF),
            ((edges, LANES), I32),
            ((depth, edges), BF),
            ((depth, edges), BF),
            ((1, rows), F32),
            ((LANES, rows // LANES), F32),
        ],
        [rel, src, src_index, dst_index, rel_index, neg_index],
        "relation_rows",
        flops=4 * depth * edges * relation_count,
        scratch=[pltpu.VMEM((depth, relation_count), BF), pltpu.SemaphoreType.DMA((4,))],
        hbm=(0,),
        limit=40,
    )
    other = moved(own, to=1)
    query_y = moved(query, to=2)
    query_c, query_cy = moved(query, to=1), moved(query_y, to=1)

    matmul = 2 * edges * rows * depth
    query1, src1, src_state1 = call(
        functools.partial(src0_kernel, negatives),
        [((tall, edges), BF), ((depth, edges), F32), ((1, edges), F32)],
        [
            own, other, query_t, target_at, count, src, src_state.reshape(1, edges),
            rel0, rel1, src_index, dst_index,
        ],
        "source_step0",
        flops=2 * matmul,
        limit=24,
    )
    next_own, next_y = moved(query1, along=-1), moved(query1, along=-1, to=2)

    block1, turned1, delta0, dst_state1, column1 = call(
        functools.partial(dst0_kernel, negatives),
        [
            ((depth, rows), BF),
            ((rows, depth), BF),
            ((depth, half), F32),
            ((1, half), F32),
            ((LANES, rows // LANES), F32),
        ],
        [own, other, query, query_y, query_c, query_cy, column, negs_next],
        "destination_step0",
        flops=8 * matmul,
        limit=32,
    )
    next_c, next_cy = moved(next_own, to=1), moved(next_y, to=1)

    delta = call(
        functools.partial(dst1_kernel, negatives),
        [((depth, half), BF)],
        [turned1, next_own, next_y, next_c, next_cy, column1, delta0, dst_state1],
        "destination_step1",
        flops=4 * matmul,
        limit=24,
    )
    home_own = moved(delta, along=-1)
    query_grad = call(
        functools.partial(query1_kernel, negatives),
        [((depth, edges), BF)],
        [turned1, block1, next_own, column1],
        "query_gradient_step1",
        flops=2 * matmul,
        limit=24,
    )
    home_grad = moved(query_grad, along=1)
    home_other = moved(home_own, to=1)
    src_out = call(
        src1_kernel,
        [((depth, edges), F32)],
        [home_grad, rel1, src1, src_state1, src_index],
        "source_step1",
        limit=16,
    )
    dst_out = call(
        final_kernel,
        [((depth, rows), F32)],
        [dst, home_own, home_other],
        "destination_out",
        limit=16,
    )
    return src_out.T, dst_out.T


def solution(mesh):
    in_specs = (
        P(("wide", "narrow"), None),
        P(("wide", "narrow")),
        P("wide", None),
        P("wide"),
        P(),
        P(("wide", "narrow"), None, None),
        P(("wide", "narrow"), None, None),
        P(("wide", "narrow"), None, None),
        P("wide", None, None),
    )
    out_specs = (P(("wide", "narrow"), None), P("wide", None))
    return jax.shard_map(body, mesh=mesh, in_specs=in_specs, out_specs=out_specs, check_vma=False)
```

```python
import functools

import jax
import jax.numpy as jnp
from jax import lax
from jax.experimental import pallas as pl
from jax.experimental.pallas import tpu as pltpu
from jax.sharding import PartitionSpec as P

LEARNING_RATE = 0.1
BF = jnp.bfloat16
F32 = jnp.float32
I32 = jnp.int32
META = 16
FINE = 32
LANES = 128
PIECE = 1920


def dot(a, b):
    return lax.dot_general(a, b, (((1,), (0,)), ((), ())), preferred_element_type=F32)


def dot_nt(a, b):
    return lax.dot_general(a, b, (((1,), (1,)), ((), ())), preferred_element_type=F32)


def core():
    return lax.rem(lax.axis_index("narrow"), 2)


def iota(shape, dim):
    return lax.broadcasted_iota(I32, shape, dim)


def one_hot(rows, index):
    return (iota((rows, index.shape[1]), 0) == index).astype(F32).astype(BF)


def eye(n):
    return (iota((n, n), 0) == iota((n, n), 1)).astype(F32).astype(BF)


def two_rows(first, second, width):
    at = iota((META, width), 0)
    return jnp.where(at == 0, first, jnp.where(at == 1, second, 0.0)).astype(BF)


def index_rows(index):
    fine = lax.rem(index, FINE)
    coarse = lax.div(index, FINE)
    return two_rows(coarse.astype(F32), fine.astype(F32), index.shape[1])


def split(value):
    high = value.astype(BF)
    return high, (value - high.astype(F32)).astype(BF)


def picked(value, hot):
    high, low = split(value)
    return dot(high, hot) + dot(low, hot)


def summed(value, hot):
    high, low = split(value)
    return dot_nt(high, hot) + dot_nt(low, hot)


def coefficients(scores, count, is_target, negatives):
    tanh = jnp.tanh(0.5 * scores)
    scale = count * (0.5 / negatives)
    pull = jnp.where(is_target, 0.5 * tanh - 0.5, 0.0)
    return (scale * tanh + scale + pull).astype(BF)


def step_size(state, gradient):
    state = state + jnp.mean(gradient * gradient, axis=0, keepdims=True)
    return state, LEARNING_RATE / jnp.sqrt(state)


def cast_kernel(emb_ref, state_ref, out_ref, held, held_state, sems):
    depth, half = held.shape
    columns = pl.ds(pl.multiple_of(core() * half, half), half)
    copy = pltpu.make_async_copy(emb_ref.at[:, columns], held, sems.at[0])
    copy_state = pltpu.make_async_copy(state_ref.at[:, columns], held_state, sems.at[1])
    copy.start()
    copy_state.start()
    copy_state.wait()
    state = held_state[...]
    high = state.astype(BF).astype(F32)
    out_ref[depth:, :] = two_rows(high, state - high, half)
    copy.wait()
    out_ref[:depth, :] = held[...].astype(BF)


def count_grid(index, blocks):
    return one_hot(blocks, lax.div(index, LANES)), one_hot(LANES, lax.rem(index, LANES))


def count_rows(index, blocks):
    coarse, fine = count_grid(index, blocks)
    return dot_nt(coarse, fine)


def prep_kernel(
    rows, rel_ref, src_ref, src_index, dst_index, rel_index, neg_index,
    q_ref, qt_ref, at_ref, rel0_ref, rel1_ref, count_ref, column_ref, next_ref,
):
    depth, edges = src_ref.shape
    relations = rel_ref.shape[1]
    blocks = rows // LANES
    flip = core() * (rows // 2)
    coarse, fine = count_grid(neg_index[0:1, :] ^ flip, blocks)
    counts = dot_nt(coarse, fine)
    for i in range(blocks):
        count_ref[:, i * LANES : (i + 1) * LANES] = counts[i : i + 1, :]
    column_ref[...] = dot_nt(fine, coarse)
    counts = count_rows(neg_index[1:2, :] ^ flip, blocks)
    high = jnp.floor(counts * (1.0 / FINE))
    next_ref[...] = jnp.concatenate([high, counts - high * FINE], axis=0)

    src_rows = picked(src_ref[...], one_hot(edges, src_index[0:1, :]))
    which = jnp.concatenate([rel_index[0:1, :], rel_index[1:2, :]], axis=1)
    block = lax.div(which, LANES)
    within = one_hot(LANES, lax.rem(which, LANES))
    found = jnp.zeros((depth, 2 * edges), F32)
    for start in range(0, relations, PIECE):
        size = min(PIECE, relations - start)
        hot = jnp.concatenate(
            [
                within * (block == start // LANES + i).astype(F32).astype(BF)
                for i in range(size // LANES)
            ],
            axis=0,
        )
        found = found + dot(rel_ref[:, start : start + size], hot)
    rel0_ref[...] = found[:, :edges].astype(BF)
    rel1_ref[...] = found[:, edges:].astype(BF)
    query = (src_rows * found[:, :edges]).astype(BF)
    meta = index_rows(dst_index[0:1, :])
    q_ref[:depth, :] = query
    q_ref[depth:, :] = meta
    turn = eye(edges)
    qt_ref[...] = dot_nt(turn, query).astype(BF)
    parts = dot_nt(turn, meta)
    local = (parts[:, 0:1] * FINE + parts[:, 1:2]).astype(I32) ^ flip
    at_ref[...] = jnp.broadcast_to(local, at_ref.shape)


def src0_kernel(
    negatives, own_ref, other_ref, qt_ref, at_ref, count_ref, src_ref, state_ref,
    rel0_ref, rel1_ref, src_index, dst_index, next_ref, q_ref, src_out, state_out,
):
    depth, edges = src_ref.shape
    half = own_ref.shape[1]
    query_grad = jnp.zeros((depth, edges), F32)
    for i, block_ref in enumerate((own_ref, other_ref)):
        block = block_ref[:depth, :]
        scores = dot(qt_ref[...], block)
        target = iota(scores.shape, 1) + i * half == at_ref[:, 0:1]
        count = count_ref[:, i * half : (i + 1) * half]
        query_grad += dot_nt(block, coefficients(scores, count, target, negatives))
    gradient = summed(
        query_grad * rel0_ref[...].astype(F32), one_hot(edges, src_index[0:1, :])
    )
    state, size = step_size(state_ref[...], gradient)
    src = src_ref[...] - gradient * size
    src_out[...] = src
    state_out[...] = state
    rows = picked(src, one_hot(edges, src_index[1:2, :]))
    q_ref[:depth, :] = (rows * rel1_ref[...].astype(F32)).astype(BF)
    blocks = next_ref.shape[0] // 2
    counts = jnp.concatenate([next_ref[:blocks, :], next_ref[blocks:, :]], axis=1)
    gap = jnp.zeros((META // 2, edges), F32)
    meta = index_rows(dst_index[1:2, :]).astype(F32)
    q_ref[depth:, :] = (meta + jnp.concatenate([gap, counts], axis=0)).astype(BF)


def targets(q_ref, depth, flip):
    parts = q_ref[depth:, :].astype(F32)
    return (parts[0:1, :] * FINE + parts[1:2, :]).astype(I32) ^ flip


def sent_counts(q_ref, depth):
    parts = dot_nt(eye(LANES), q_ref[depth:, :LANES]) * FINE
    parts = parts + dot_nt(eye(LANES), q_ref[depth:, LANES : 2 * LANES])
    return parts[:, META // 2 :]


def row_coefficients(block_t, start, q_ref, column, flip, negatives):
    rows, depth = block_t.shape
    scores = dot(block_t, q_ref[:depth, :])
    target = iota(scores.shape, 0) + start == targets(q_ref, depth, flip)
    first = start // LANES
    count = jnp.concatenate(
        [column[:, first + i : first + i + 1] for i in range(rows // LANES)], axis=0
    )
    return coefficients(scores, count, target, negatives)


def dst_gradient(block_t, start, q_refs, column, flip, negatives):
    rows, depth = block_t.shape
    total = jnp.zeros((depth, rows), F32)
    for q_ref in q_refs:
        weights = row_coefficients(block_t, start, q_ref, column, flip, negatives)
        total += dot_nt(q_ref[:depth, :], weights)
    return total


def dst0_kernel(
    negatives, own_ref, other_ref, qa, qb, qc, qd, column_ref,
    block_out, turned_out, delta_out, state_out,
):
    depth, half = delta_out.shape
    flip = core() * half
    turn = eye(2 * LANES)
    column = column_ref[...]
    for i, block_ref in enumerate((own_ref, other_ref)):
        block = block_ref[:depth, :]
        turned = jnp.concatenate(
            [
                dot_nt(turn, block[:, k : k + 2 * LANES]).astype(BF)
                for k in range(0, half, 2 * LANES)
            ],
            axis=0,
        )
        gradient = dst_gradient(turned, i * half, (qa, qb, qc, qd), column, flip, negatives)
        parts = block_ref[depth:, :].astype(F32)
        state, size = step_size(parts[0:1, :] + parts[1:2, :], gradient)
        delta = gradient * size
        block = (block.astype(F32) - delta).astype(BF)
        block_out[:, i * half : (i + 1) * half] = block
        for k in range(0, half, 2 * LANES):
            turned_out[i * half + k : i * half + k + 2 * LANES, :] = dot_nt(
                turn, block[:, k : k + 2 * LANES]
            ).astype(BF)
        if i == 0:
            delta_out[...] = delta
            state_out[...] = state


def dst1_kernel(
    negatives, turned_ref, qa, qb, qc, qd, delta_ref, state_ref, delta_out
):
    depth, half = delta_ref.shape
    flip = core() * half
    gradient = dst_gradient(
        turned_ref[:half, :], 0, (qa, qb, qc, qd), sent_counts(qa, depth), flip, negatives
    )
    _, size = step_size(state_ref[...], gradient)
    delta_out[...] = (delta_ref[...] + gradient * size).astype(BF)


def query1_kernel(negatives, turned_ref, block_ref, q_ref, out_ref):
    rows, depth = turned_ref.shape
    weights = row_coefficients(
        turned_ref[...], 0, q_ref, sent_counts(q_ref, depth), core() * (rows // 2), negatives
    )
    out_ref[...] = dot(block_ref[...], weights).astype(BF)


def src1_kernel(grad_ref, rel_ref, src_ref, state_ref, src_index, src_out):
    edges = src_ref.shape[1]
    gradient = summed(
        grad_ref[...].astype(F32) * rel_ref[...].astype(F32), one_hot(edges, src_index[1:2, :])
    )
    _, size = step_size(state_ref[...], gradient)
    src_out[...] = src_ref[...] - gradient * size


def final_kernel(emb_ref, own_ref, other_ref, out_ref):
    half = own_ref.shape[1]
    here = core()
    for place, delta_ref in ((here, own_ref), (1 - here, other_ref)):
        columns = pl.ds(pl.multiple_of(place * half, half), half)
        out_ref[:, columns] = emb_ref[:, columns] - delta_ref[...].astype(F32)


def call(kernel, outs, args, name, flops=0, scratch=(), hbm=(), limit=32):
    vmem = pl.BlockSpec(memory_space=pltpu.VMEM)
    anywhere = pl.BlockSpec(memory_space=pl.ANY)
    shapes = [jax.ShapeDtypeStruct(shape, dtype) for shape, dtype in outs]
    size = sum(a.size * a.dtype.itemsize for a in [*args, *shapes])
    result = pl.pallas_call(
        kernel,
        out_shape=shapes,
        in_specs=[anywhere if i in hbm else vmem for i in range(len(args))],
        out_specs=[vmem] * len(shapes),
        scratch_shapes=list(scratch),
        compiler_params=pltpu.CompilerParams(vmem_limit_bytes=limit << 20),
        cost_estimate=pl.CostEstimate(flops=flops, bytes_accessed=size, transcendentals=0),
        name=name,
    )(*args)
    return result[0] if len(shapes) == 1 else result


def body(
    src_emb, src_state, dst_emb, dst_state, relations, src_index, dst_index, rel_index, neg_index
):
    wide, narrow = lax.axis_size("wide"), lax.axis_size("narrow")

    def moved(value, along=0, to=0):
        pairs = [
            (w * narrow + n, ((w + along) % wide) * narrow + (n ^ to))
            for w in range(wide)
            for n in range(narrow)
        ]
        return lax.ppermute(value, ("wide", "narrow"), pairs)

    rows, depth = dst_emb.shape
    edges = src_emb.shape[0]
    half = rows // 2
    src_index, dst_index, rel_index, neg_index = (
        a[0] for a in (src_index, dst_index, rel_index, neg_index)
    )
    negatives = neg_index.shape[1]
    dst, src, rel = dst_emb.T, src_emb.T, relations.T
    tall = depth + META

    payload = call(
        cast_kernel,
        [((tall, half), BF)],
        [dst, dst_state.reshape(1, rows)],
        "cast_block",
        scratch=[
            pltpu.VMEM((depth, half), F32),
            pltpu.VMEM((1, half), F32),
            pltpu.SemaphoreType.DMA((2,)),
        ],
        hbm=(0, 1),
        limit=60,
    )
    own = moved(payload, along=1)
    rel, payload = lax.optimization_barrier((rel, payload))

    src_state = src_state.reshape(1, edges)
    blocks = rows // LANES
    query, query_t, target_at, rel0, rel1, count, column, count1 = call(
        functools.partial(prep_kernel, rows),
        [
            ((tall, edges), BF),
            ((edges, depth), BF),
            ((edges, LANES), I32),
            ((depth, edges), BF),
            ((depth, edges), BF),
            ((1, rows), F32),
            ((LANES, blocks), F32),
            ((2 * blocks, LANES), F32),
        ],
        [rel, src, src_index, dst_index, rel_index, neg_index],
        "relation_rows",
        flops=4 * depth * edges * relations.shape[0],
        limit=32,
    )
    query_c, query_y = moved(query, to=1), moved(query, to=2)
    own, query_y, query_c = lax.optimization_barrier((own, query_y, query_c))
    other = moved(own, to=1)
    query_cy = moved(query_y, to=1)

    matmul = 2 * edges * rows * depth
    query1, src1, src_state1 = call(
        functools.partial(src0_kernel, negatives),
        [((tall, edges), BF), ((depth, edges), F32), ((1, edges), F32)],
        [
            own, other, query_t, target_at, count, src, src_state,
            rel0, rel1, src_index, dst_index, count1,
        ],
        "source_step0",
        flops=2 * matmul,
        limit=24,
    )
    next_own, next_y = moved(query1, along=-1), moved(query1, along=-1, to=2)
    own, query1 = lax.optimization_barrier((own, query1))

    block1, turned1, delta0, dst_state1 = call(
        functools.partial(dst0_kernel, negatives),
        [
            ((depth, rows), BF),
            ((rows, depth), BF),
            ((depth, half), F32),
            ((1, half), F32),
        ],
        [own, other, query, query_y, query_c, query_cy, column],
        "destination_step0",
        flops=8 * matmul,
        limit=32,
    )
    next_own, next_y, block1 = lax.optimization_barrier((next_own, next_y, block1))
    next_c, next_cy = moved(next_own, to=1), moved(next_y, to=1)

    delta = call(
        functools.partial(dst1_kernel, negatives),
        [((depth, half), BF)],
        [turned1, next_own, next_y, next_c, next_cy, delta0, dst_state1],
        "destination_step1",
        flops=4 * matmul,
        limit=24,
    )
    home_own = moved(delta, along=-1)
    block1, delta = lax.optimization_barrier((block1, delta))
    query_grad = call(
        functools.partial(query1_kernel, negatives),
        [((depth, edges), BF)],
        [turned1, block1, next_own],
        "query_gradient_step1",
        flops=2 * matmul,
        limit=24,
    )
    home_grad = moved(query_grad, along=1)
    src_out = call(
        src1_kernel,
        [((depth, edges), F32)],
        [home_grad, rel1, src1, src_state1, src_index],
        "source_step1",
        limit=16,
    )
    home_own, src_out = lax.optimization_barrier((home_own, src_out))
    home_other = moved(home_own, to=1)
    dst_out = call(
        final_kernel,
        [((depth, rows), F32)],
        [dst, home_own, home_other],
        "destination_out",
        limit=16,
    )
    return src_out.T, dst_out.T


def solution(mesh):
    in_specs = (
        P(("wide", "narrow"), None),
        P(("wide", "narrow")),
        P("wide", None),
        P("wide"),
        P(),
        P(("wide", "narrow"), None, None),
        P(("wide", "narrow"), None, None),
        P(("wide", "narrow"), None, None),
        P("wide", None, None),
    )
    out_specs = (P(("wide", "narrow"), None), P("wide", None))
    return jax.shard_map(body, mesh=mesh, in_specs=in_specs, out_specs=out_specs, check_vma=False)
```

```python
import functools

import jax
import jax.numpy as jnp
from jax import lax
from jax.experimental import pallas as pl
from jax.experimental.pallas import tpu as pltpu
from jax.sharding import PartitionSpec as P

LEARNING_RATE = 0.1
BF = jnp.bfloat16
F32 = jnp.float32
I32 = jnp.int32
META = 16
FINE = 32
LANES = 128
PIECE = 1920


def dot(a, b):
    return lax.dot_general(a, b, (((1,), (0,)), ((), ())), preferred_element_type=F32)


def dot_nt(a, b):
    return lax.dot_general(a, b, (((1,), (1,)), ((), ())), preferred_element_type=F32)


def core():
    return lax.rem(lax.axis_index("narrow"), 2)


def iota(shape, dim):
    return lax.broadcasted_iota(I32, shape, dim)


def one_hot(rows, index):
    return (iota((rows, index.shape[1]), 0) == index).astype(F32).astype(BF)


def eye(n):
    return (iota((n, n), 0) == iota((n, n), 1)).astype(F32).astype(BF)


def two_rows(first, second, width):
    at = iota((META, width), 0)
    return jnp.where(at == 0, first, jnp.where(at == 1, second, 0.0)).astype(BF)


def index_rows(index):
    fine = lax.rem(index, FINE)
    coarse = lax.div(index, FINE)
    return two_rows(coarse.astype(F32), fine.astype(F32), index.shape[1])


def split(value):
    high = value.astype(BF)
    return high, (value - high.astype(F32)).astype(BF)


def picked(value, hot):
    high, low = split(value)
    return dot(high, hot) + dot(low, hot)


def summed(value, hot):
    high, low = split(value)
    return dot_nt(high, hot) + dot_nt(low, hot)


def coefficients(scores, count, is_target, negatives):
    tanh = jnp.tanh(0.5 * scores)
    scale = count * (0.5 / negatives)
    pull = jnp.where(is_target, 0.5 * tanh - 0.5, 0.0)
    return (scale * tanh + scale + pull).astype(BF)


def step_size(state, gradient):
    state = state + jnp.mean(gradient * gradient, axis=0, keepdims=True)
    return state, LEARNING_RATE / jnp.sqrt(state)


def cast_kernel(emb_ref, state_ref, out_ref, held, held_state, sems):
    depth, half = held.shape
    columns = pl.ds(pl.multiple_of(core() * half, half), half)
    copy_state = pltpu.make_async_copy(state_ref.at[:, columns], held_state, sems.at[0])
    copies = []
    for i, start in enumerate(range(0, depth, depth // 5)):
        part = pl.ds(start, depth // 5)
        copy = pltpu.make_async_copy(emb_ref.at[part, columns], held.at[part], sems.at[i + 1])
        copy.start()
        copies.append((copy, part))
    copy_state.start()
    for copy, part in copies:
        copy.wait()
        out_ref[part, :] = held[part, :].astype(BF)
    copy_state.wait()
    state = held_state[...]
    high = state.astype(BF).astype(F32)
    out_ref[depth:, :] = two_rows(high, state - high, half)


def count_grid(index, blocks):
    return one_hot(blocks, lax.div(index, LANES)), one_hot(LANES, lax.rem(index, LANES))


def relation_rows(rel_ref, index):
    depth, relations = rel_ref.shape
    block = lax.div(index, LANES)
    within = one_hot(LANES, lax.rem(index, LANES))
    found = jnp.zeros((depth, index.shape[1]), F32)
    for start in range(0, relations, PIECE):
        size = min(PIECE, relations - start)
        hot = jnp.concatenate(
            [
                within * (block == start // LANES + i).astype(F32).astype(BF)
                for i in range(size // LANES)
            ],
            axis=0,
        )
        found = found + dot(rel_ref[:, start : start + size], hot)
    return found


def lane_row(counts, out_ref):
    for i in range(counts.shape[0]):
        out_ref[:, i * LANES : (i + 1) * LANES] = counts[i : i + 1, :]


def query0_kernel(
    rel_ref, src_ref, src_index, dst_index, rel_index, q_ref, rel_out
):
    depth, edges = src_ref.shape
    found = relation_rows(rel_ref, rel_index[0:1, :])
    rel_out[...] = found.astype(BF)
    rows = picked(src_ref[...], one_hot(edges, src_index[0:1, :]))
    q_ref[:depth, :] = (rows * found).astype(BF)
    q_ref[depth:, :] = index_rows(dst_index[0:1, :])


def prep_kernel(
    rows, rel_ref, q_ref, rel_index, neg_index,
    qt_ref, at_ref, rel_out, count_ref, column_ref, next_ref, next_count_ref,
):
    depth, edges = rel_out.shape
    blocks = rows // LANES
    flip = core() * (rows // 2)
    coarse, fine = count_grid(neg_index[0:1, :] ^ flip, blocks)
    lane_row(dot_nt(coarse, fine), count_ref)
    column_ref[...] = dot_nt(fine, coarse)
    coarse, fine = count_grid(neg_index[1:2, :] ^ flip, blocks)
    counts = dot_nt(coarse, fine)
    high = jnp.floor(counts * (1.0 / FINE))
    next_ref[...] = jnp.concatenate([high, counts - high * FINE], axis=0)
    lane_row(counts, next_count_ref)
    rel_out[...] = relation_rows(rel_ref, rel_index[1:2, :]).astype(BF)
    query_t, target_at = turned_query(q_ref, depth, flip)
    qt_ref[...] = query_t
    at_ref[...] = jnp.broadcast_to(target_at, at_ref.shape)


def turned_query(q_ref, depth, flip):
    turn = eye(q_ref.shape[1])
    parts = dot_nt(turn, q_ref[depth:, :])
    target_at = (parts[:, 0:1] * FINE + parts[:, 1:2]).astype(I32) ^ flip
    return dot_nt(turn, q_ref[:depth, :]).astype(BF), target_at


def query_gradient(negatives, blocks, query_t, target_at, count_ref):
    total = 0.0
    start = 0
    for block in blocks:
        rows = block.shape[1]
        scores = dot(query_t, block)
        target = iota(scores.shape, 1) + start == target_at
        count = count_ref[:, start : start + rows]
        total += dot_nt(block, coefficients(scores, count, target, negatives))
        start += rows
    return total


def src0_kernel(
    negatives, own_ref, other_ref, qt_ref, at_ref, count_ref, src_ref, state_ref,
    rel0_ref, rel1_ref, src_index, dst_index, next_ref, q_ref, src_out, state_out,
):
    depth, edges = src_ref.shape
    blocks = own_ref[:depth, :], other_ref[:depth, :]
    grad = query_gradient(negatives, blocks, qt_ref[...], at_ref[:, 0:1], count_ref)
    gradient = summed(grad * rel0_ref[...].astype(F32), one_hot(edges, src_index[0:1, :]))
    state, size = step_size(state_ref[...], gradient)
    src = src_ref[...] - gradient * size
    src_out[...] = src
    state_out[...] = state
    rows = picked(src, one_hot(edges, src_index[1:2, :]))
    q_ref[:depth, :] = (rows * rel1_ref[...].astype(F32)).astype(BF)
    blocks = next_ref.shape[0] // 2
    counts = jnp.concatenate([next_ref[:blocks, :], next_ref[blocks:, :]], axis=1)
    gap = jnp.zeros((META // 2, edges), F32)
    meta = index_rows(dst_index[1:2, :]).astype(F32)
    q_ref[depth:, :] = (meta + jnp.concatenate([gap, counts], axis=0)).astype(BF)


def src1_kernel(
    negatives, own_ref, other_ref, last_ref, q_ref, count_ref, src_ref, state_ref, rel_ref,
    src_index, src_out,
):
    depth, edges = src_ref.shape
    half = own_ref.shape[1]
    query_t, target_at = turned_query(q_ref, depth, core() * half)
    blocks = own_ref[...], other_ref[...], last_ref[...]
    grad = query_gradient(negatives, blocks, query_t, target_at, count_ref)
    gradient = summed(grad * rel_ref[...].astype(F32), one_hot(edges, src_index[1:2, :]))
    _, size = step_size(state_ref[...], gradient)
    src_out[...] = src_ref[...] - gradient * size


def targets(q_ref, depth, flip):
    parts = q_ref[depth:, :].astype(F32)
    return (parts[0:1, :] * FINE + parts[1:2, :]).astype(I32) ^ flip


def sent_counts(q_ref, depth):
    parts = dot_nt(eye(LANES), q_ref[depth:, :LANES]) * FINE
    parts = parts + dot_nt(eye(LANES), q_ref[depth:, LANES : 2 * LANES])
    return parts[:, META // 2 :]


def row_coefficients(block_t, start, q_ref, column, flip, negatives):
    rows, depth = block_t.shape
    scores = dot(block_t, q_ref[:depth, :])
    target = iota(scores.shape, 0) + start == targets(q_ref, depth, flip)
    first = start // LANES
    count = jnp.concatenate(
        [column[:, first + i : first + i + 1] for i in range(rows // LANES)], axis=0
    )
    return coefficients(scores, count, target, negatives)


def dst_gradient(block_t, q_refs, column, flip, negatives):
    rows, depth = block_t.shape
    total = jnp.zeros((depth, rows), F32)
    for q_ref in q_refs:
        weights = row_coefficients(block_t, 0, q_ref, column, flip, negatives)
        total += dot_nt(q_ref[:depth, :], weights)
    return total


def turned(block):
    step = 2 * LANES
    turn = eye(step)
    return jnp.concatenate(
        [dot_nt(turn, block[:, k : k + step]).astype(BF) for k in range(0, block.shape[1], step)],
        axis=0,
    )


def dst0_kernel(
    negatives, own_ref, qa, qb, qc, qd, column_ref,
    block_out, turned_out, delta_out, state_out,
):
    depth, half = delta_out.shape
    block = own_ref[:depth, :]
    queries = qa, qb, qc, qd
    gradient = dst_gradient(
        turned(block), queries, column_ref[...], core() * half, negatives
    )
    parts = own_ref[depth:, :].astype(F32)
    state, size = step_size(parts[0:1, :] + parts[1:2, :], gradient)
    delta = gradient * size
    block = (block.astype(F32) - delta).astype(BF)
    block_out[...] = block
    turned_out[...] = turned(block)
    delta_out[...] = delta
    state_out[...] = state


def dst1_kernel(
    negatives, turned_ref, qa, qb, qc, qd, delta_ref, state_ref, delta_out
):
    depth, half = delta_ref.shape
    gradient = dst_gradient(
        turned_ref[...], (qa, qb, qc, qd), sent_counts(qa, depth), core() * half, negatives
    )
    _, size = step_size(state_ref[...], gradient)
    delta_out[:depth, :] = (delta_ref[...] + gradient * size).astype(BF)
    delta_out[depth:, :] = jnp.zeros((META, half), BF)


def final_kernel(emb_ref, own_ref, other_ref, out_ref):
    depth, half = emb_ref.shape[0], own_ref.shape[1]
    here = core()
    for place, delta_ref in ((here, own_ref), (1 - here, other_ref)):
        columns = pl.ds(pl.multiple_of(place * half, half), half)
        out_ref[:, columns] = emb_ref[:, columns] - delta_ref[:depth, :].astype(F32)


def call(kernel, outs, args, name, flops=None, scratch=(), hbm=(), limit=32):
    vmem = pl.BlockSpec(memory_space=pltpu.VMEM)
    anywhere = pl.BlockSpec(memory_space=pltpu.HBM)
    shapes = [jax.ShapeDtypeStruct(shape, dtype) for shape, dtype in outs]
    size = sum(a.size * a.dtype.itemsize for a in [*args, *shapes])
    result = pl.pallas_call(
        kernel,
        out_shape=shapes,
        in_specs=[anywhere if i in hbm else vmem for i in range(len(args))],
        out_specs=[vmem] * len(shapes),
        scratch_shapes=list(scratch),
        compiler_params=pltpu.CompilerParams(vmem_limit_bytes=int(limit * 2**20)),
        cost_estimate=pl.CostEstimate(
            flops=flops or 1, bytes_accessed=size if flops else 1, transcendentals=0
        ),
        name=name,
    )(*args)
    return result[0] if len(shapes) == 1 else result


def body(
    src_emb, src_state, dst_emb, dst_state, relations, src_index, dst_index, rel_index, neg_index
):
    wide, narrow = lax.axis_size("wide"), lax.axis_size("narrow")

    def moved(value, along=0, to=0):
        pairs = [
            (w * narrow + n, ((w + along) % wide) * narrow + (n ^ to))
            for w in range(wide)
            for n in range(narrow)
        ]
        return lax.ppermute(value, ("wide", "narrow"), pairs)

    rows, depth = dst_emb.shape
    edges = src_emb.shape[0]
    half = rows // 2
    src_index, dst_index, rel_index, neg_index = (
        a[0] for a in (src_index, dst_index, rel_index, neg_index)
    )
    negatives = neg_index.shape[1]
    dst, src, rel = dst_emb.T, src_emb.T, relations.T
    tall = depth + META

    payload = call(
        cast_kernel,
        [((tall, half), BF)],
        [dst, dst_state.reshape(1, rows)],
        "cast_block",
        scratch=[
            pltpu.VMEM((depth, half), F32),
            pltpu.VMEM((1, half), F32),
            pltpu.SemaphoreType.DMA((6,)),
        ],
        hbm=(0, 1),
        limit=8,
    )
    own = moved(payload, along=1)
    src_index, payload = lax.optimization_barrier((src_index, payload))

    src_state = src_state.reshape(1, edges)
    blocks = rows // LANES
    matmul = 2 * edges * rows * depth
    table = 2 * edges * relations.shape[0] * depth
    query, rel0 = call(
        query0_kernel,
        [((tall, edges), BF), ((depth, edges), BF)],
        [rel, src, src_index, dst_index, rel_index],
        "query_step0",
        flops=table,
        limit=32,
    )
    query_c, query_y = moved(query, to=1), moved(query, to=2)
    query_t, target_at, rel1, count0, column, counts_sent, count1 = call(
        functools.partial(prep_kernel, rows),
        [
            ((edges, depth), BF),
            ((edges, LANES), I32),
            ((depth, edges), BF),
            ((1, rows), F32),
            ((LANES, blocks), F32),
            ((2 * blocks, LANES), F32),
            ((1, rows), F32),
        ],
        [rel, query, rel_index, neg_index],
        "prepare",
        flops=table,
        limit=32,
    )
    own, query_y, query_c, rel1 = lax.optimization_barrier((own, query_y, query_c, rel1))
    other = moved(own, to=1)
    query_cy = moved(query_y, to=1)

    query1, src1, src_state1 = call(
        functools.partial(src0_kernel, negatives),
        [((tall, edges), BF), ((depth, edges), F32), ((1, edges), F32)],
        [
            own, other, query_t, target_at, count0, src, src_state,
            rel0, rel1, src_index, dst_index, counts_sent,
        ],
        "source_step0",
        flops=2 * matmul,
        limit=24,
    )
    next_own, next_y = moved(query1, along=-1), moved(query1, along=-1, to=2)
    own, query1 = lax.optimization_barrier((own, query1))

    block1, turned1, delta0, dst_state1 = call(
        functools.partial(dst0_kernel, negatives),
        [((depth, half), BF), ((half, depth), BF), ((depth, half), F32), ((1, half), F32)],
        [own, query, query_y, query_c, query_cy, column],
        "destination_step0",
        limit=24,
    )
    block1_own = moved(block1, along=1)
    next_own, next_y, block1 = lax.optimization_barrier((next_own, next_y, block1))
    next_c, next_cy = moved(next_own, to=1), moved(next_y, to=1)

    delta = call(
        functools.partial(dst1_kernel, negatives),
        [((tall, half), BF)],
        [turned1, next_own, next_y, next_c, next_cy, delta0, dst_state1],
        "destination_step1",
        flops=4 * matmul,
        limit=24,
    )
    home_own = moved(delta, along=-1)

    block1_own, delta = lax.optimization_barrier((block1_own, delta))
    block1_other = [moved(block1_own[:, k : k + half // 2], to=1) for k in (0, half // 2)]
    src_out = call(
        functools.partial(src1_kernel, negatives),
        [((depth, edges), F32)],
        [block1_own, *block1_other, query1, count1, src1, src_state1, rel1, src_index],
        "source_step1",
        limit=24,
    )
    home_own, src_out = lax.optimization_barrier((home_own, src_out))
    home_other = moved(home_own, to=1)
    dst_out = call(
        final_kernel,
        [((depth, rows), F32)],
        [dst, home_own, home_other],
        "destination_out",
        limit=16,
    )
    return src_out.T, dst_out.T


def solution(mesh):
    in_specs = (
        P(("wide", "narrow"), None),
        P(("wide", "narrow")),
        P("wide", None),
        P("wide"),
        P(),
        P(("wide", "narrow"), None, None),
        P(("wide", "narrow"), None, None),
        P(("wide", "narrow"), None, None),
        P("wide", None, None),
    )
    out_specs = (P(("wide", "narrow"), None), P("wide", None))
    return jax.shard_map(body, mesh=mesh, in_specs=in_specs, out_specs=out_specs, check_vma=False)
```

```python
import functools

import jax
import jax.numpy as jnp
from jax import lax
from jax.experimental import pallas as pl
from jax.experimental.pallas import tpu as pltpu
from jax.sharding import PartitionSpec as P

LEARNING_RATE = 0.1
BF = jnp.bfloat16
F32 = jnp.float32
I32 = jnp.int32
META = 16
FINE = 32
LANES = 128
PIECE = 1920


def dot(a, b):
    return lax.dot_general(a, b, (((1,), (0,)), ((), ())), preferred_element_type=F32)


def dot_nt(a, b):
    return lax.dot_general(a, b, (((1,), (1,)), ((), ())), preferred_element_type=F32)


def core():
    return lax.rem(lax.axis_index("narrow"), 2)


def iota(shape, dim):
    return lax.broadcasted_iota(I32, shape, dim)


def one_hot(rows, index):
    return (iota((rows, index.shape[1]), 0) == index).astype(F32).astype(BF)


def eye(n):
    return (iota((n, n), 0) == iota((n, n), 1)).astype(F32).astype(BF)


def index_rows(index):
    fine = lax.rem(index, FINE)
    coarse = lax.div(index, FINE)
    at = iota((META, index.shape[1]), 0)
    parts = jnp.where(at == 0, coarse, jnp.where(at == 1, fine, 0))
    return parts.astype(F32).astype(BF)


def split(value):
    high = value.astype(BF)
    return high, (value - high.astype(F32)).astype(BF)


def picked(value, hot):
    high, low = split(value)
    return dot(high, hot) + dot(low, hot)


def summed(value, hot):
    high, low = split(value)
    return dot_nt(high, hot) + dot_nt(low, hot)


def coefficients(scores, count, is_target, negatives):
    tanh = jnp.tanh(0.5 * scores)
    scale = count * (0.5 / negatives)
    pull = jnp.where(is_target, 0.5 * tanh - 0.5, 0.0)
    return (scale * tanh + scale + pull).astype(BF)


def step_size(state, gradient):
    state = state + jnp.mean(gradient * gradient, axis=0, keepdims=True)
    return state, LEARNING_RATE / jnp.sqrt(state)


def count_grid(index, blocks):
    return one_hot(blocks, lax.div(index, LANES)), one_hot(LANES, lax.rem(index, LANES))


def relation_rows(rel_ref, index):
    depth, relations = rel_ref.shape
    block = lax.div(index, LANES)
    within = one_hot(LANES, lax.rem(index, LANES))
    found = jnp.zeros((depth, index.shape[1]), F32)
    for start in range(0, relations, PIECE):
        size = min(PIECE, relations - start)
        hot = jnp.concatenate(
            [
                within * (block == start // LANES + i).astype(F32).astype(BF)
                for i in range(size // LANES)
            ],
            axis=0,
        )
        found = found + dot(rel_ref[:, start : start + size], hot)
    return found


def lane_row(counts, out_ref):
    for i in range(counts.shape[0]):
        out_ref[:, i * LANES : (i + 1) * LANES] = counts[i : i + 1, :]


def query0_kernel(
    rel_ref, src_ref, index, q_ref, rel_out
):
    depth, edges = src_ref.shape
    src_index, dst_index, rel_index = index[0:1, :], index[2:3, :], index[4:5, :]
    found = relation_rows(rel_ref, rel_index)
    rel_out[...] = found.astype(BF)
    rows = picked(src_ref[...], one_hot(edges, src_index))
    q_ref[:depth, :] = (rows * found).astype(BF)
    q_ref[depth:, :] = index_rows(dst_index)


def prep_kernel(
    rows, rel_ref, q_ref, rel_index, neg_index, src_ref, state_ref, src_index, dst_index,
    qt_ref, at_ref, rel_out, count_ref, column_ref, next_ref, next_count_ref,
    src_out, state_out, src_index_out, dst_index_out,
):
    depth, edges = rel_out.shape
    src_out[...] = src_ref[...]
    state_out[...] = state_ref[...]
    src_index_out[...] = src_index[...]
    dst_index_out[...] = dst_index[...]
    blocks = rows // LANES
    flip = core() * (rows // 2)
    coarse, fine = count_grid(neg_index[0:1, :] ^ flip, blocks)
    lane_row(dot_nt(coarse, fine), count_ref)
    column_ref[...] = dot_nt(fine, coarse)
    coarse, fine = count_grid(neg_index[1:2, :] ^ flip, blocks)
    counts = dot_nt(coarse, fine)
    high = jnp.floor(counts * (1.0 / FINE))
    next_ref[...] = jnp.concatenate([high, counts - high * FINE], axis=0)
    lane_row(counts, next_count_ref)
    rel_out[...] = relation_rows(rel_ref, rel_index[1:2, :]).astype(BF)
    query_t, target_at = turned_query(q_ref, depth, flip)
    qt_ref[...] = query_t
    at_ref[...] = jnp.broadcast_to(target_at, at_ref.shape)


def turned_query(q_ref, depth, flip):
    turn = eye(q_ref.shape[1])
    parts = dot_nt(turn, q_ref[depth:, :])
    target_at = (parts[:, 0:1] * FINE + parts[:, 1:2]).astype(I32) ^ flip
    return dot_nt(turn, q_ref[:depth, :]).astype(BF), target_at


def query_gradient(negatives, blocks, query_t, target_at, count_ref):
    total = 0.0
    start = 0
    for block in blocks:
        rows = block.shape[1]
        scores = dot(query_t, block)
        target = iota(scores.shape, 1) + start == target_at
        count = count_ref[:, start : start + rows]
        total += dot_nt(block, coefficients(scores, count, target, negatives))
        start += rows
    return total


def src0_kernel(
    negatives, own_ref, other_a, other_b, qt_ref, at_ref, count_ref, src_ref, state_ref,
    rel0_ref, rel1_ref, src_index, dst_index, next_ref, q_ref, src_out, state_out,
):
    depth, edges = src_ref.shape
    blocks = own_ref[...], jnp.concatenate([other_a[...], other_b[...]], axis=1)
    grad = query_gradient(negatives, blocks, qt_ref[...], at_ref[:, 0:1], count_ref)
    gradient = summed(grad * rel0_ref[...].astype(F32), one_hot(edges, src_index[0:1, :]))
    state, size = step_size(state_ref[...], gradient)
    src = src_ref[...] - gradient * size
    src_out[...] = src
    state_out[...] = state
    rows = picked(src, one_hot(edges, src_index[1:2, :]))
    q_ref[:depth, :] = (rows * rel1_ref[...].astype(F32)).astype(BF)
    blocks = next_ref.shape[0] // 2
    counts = jnp.concatenate([next_ref[:blocks, :], next_ref[blocks:, :]], axis=1)
    gap = jnp.zeros((META // 2, edges), F32)
    meta = index_rows(dst_index[1:2, :]).astype(F32)
    q_ref[depth:, :] = (meta + jnp.concatenate([gap, counts], axis=0)).astype(BF)


def src1_kernel(
    negatives, own_ref, other_ref, last_ref, q_ref, count_ref, src_ref, state_ref, rel_ref,
    src_index, src_out,
):
    depth, edges = src_ref.shape
    half = own_ref.shape[1]
    query_t, target_at = turned_query(q_ref, depth, core() * half)
    blocks = own_ref[...], other_ref[...], last_ref[...]
    grad = query_gradient(negatives, blocks, query_t, target_at, count_ref)
    gradient = summed(grad * rel_ref[...].astype(F32), one_hot(edges, src_index[1:2, :]))
    _, size = step_size(state_ref[...], gradient)
    src_out[...] = src_ref[...] - gradient * size


def targets(q_ref, depth, flip):
    parts = q_ref[depth:, :].astype(F32)
    return (parts[0:1, :] * FINE + parts[1:2, :]).astype(I32) ^ flip


def sent_counts(q_ref, depth):
    parts = dot_nt(eye(LANES), q_ref[depth:, :LANES]) * FINE
    parts = parts + dot_nt(eye(LANES), q_ref[depth:, LANES : 2 * LANES])
    return parts[:, META // 2 :]


def row_coefficients(block_t, start, q_ref, column, flip, negatives):
    rows, depth = block_t.shape
    scores = dot(block_t, q_ref[:depth, :])
    target = iota(scores.shape, 0) + start == targets(q_ref, depth, flip)
    first = start // LANES
    count = jnp.concatenate(
        [column[:, first + i : first + i + 1] for i in range(rows // LANES)], axis=0
    )
    return coefficients(scores, count, target, negatives)


def dst_gradient(block_t, q_refs, column, flip, negatives):
    rows, depth = block_t.shape
    total = jnp.zeros((depth, rows), F32)
    for q_ref in q_refs:
        weights = row_coefficients(block_t, 0, q_ref, column, flip, negatives)
        total += dot_nt(q_ref[:depth, :], weights)
    return total


def turned(block):
    step = 2 * LANES
    turn = eye(step)
    return jnp.concatenate(
        [dot_nt(turn, block[:, k : k + step]).astype(BF) for k in range(0, block.shape[1], step)],
        axis=0,
    )


def dst0_kernel(
    negatives, own_ref, old_ref, qa, qb, qc, qd, column_ref,
    block_out, turned_out, delta_out, state_out,
):
    depth, half = delta_out.shape
    block = own_ref[...]
    columns = pl.ds(pl.multiple_of(core() * half, half), half)
    queries = qa, qb, qc, qd
    gradient = dst_gradient(
        turned(block), queries, column_ref[...], core() * half, negatives
    )
    state, size = step_size(old_ref[:, columns], gradient)
    delta = gradient * size
    block = (block.astype(F32) - delta).astype(BF)
    block_out[...] = block
    turned_out[...] = turned(block)
    delta_out[...] = delta
    state_out[...] = state


def dst1_first_kernel(negatives, turned_ref, qa, qb, grad_out):
    depth, half = grad_out.shape
    grad_out[...] = dst_gradient(
        turned_ref[...], (qa, qb), sent_counts(qa, depth), core() * half, negatives
    )


def dst1_kernel(
    negatives, turned_ref, first_ref, qa, qc, qd, delta_ref, state_ref, delta_out
):
    depth, half = delta_ref.shape
    gradient = first_ref[...] + dst_gradient(
        turned_ref[...], (qc, qd), sent_counts(qa, depth), core() * half, negatives
    )
    _, size = step_size(state_ref[...], gradient)
    delta_out[:depth, :] = (delta_ref[...] + gradient * size).astype(BF)
    delta_out[depth:, :] = jnp.zeros((META, half), BF)


def final_kernel(mine, emb_ref, delta_ref, *refs):
    out_ref, held, sems = refs[-3:]
    depth, half = held.shape
    place = core() if mine else 1 - core()
    copies = []
    for i in range(2):
        size = half // 2
        columns = pl.ds(pl.multiple_of(place * half + i * size, size), size)
        part = slice(i * size, (i + 1) * size)
        held[:, part] = emb_ref[:, columns] - delta_ref[:depth, part].astype(F32)
        copies.append(
            pltpu.make_async_copy(held.at[:, part], out_ref.at[:, columns], sems.at[i])
        )
        copies[-1].start()
    for copy in copies:
        copy.wait()


def call(kernel, outs, args, name, flops=None, scratch=(), hbm=(), limit=32, out=None):
    vmem = pl.BlockSpec(memory_space=pltpu.VMEM)
    anywhere = pl.BlockSpec(memory_space=pltpu.HBM)
    shapes = [jax.ShapeDtypeStruct(shape, dtype) for shape, dtype in outs]
    size = sum(a.size * a.dtype.itemsize for a in [*args, *shapes])
    result = pl.pallas_call(
        kernel,
        out_shape=shapes,
        in_specs=[anywhere if i in hbm else vmem for i in range(len(args))],
        out_specs=[vmem if out is None else anywhere] * len(shapes),
        input_output_aliases={out: 0} if out else {},
        scratch_shapes=list(scratch),
        compiler_params=pltpu.CompilerParams(vmem_limit_bytes=int(limit * 2**20)),
        cost_estimate=pl.CostEstimate(
            flops=flops or 1, bytes_accessed=size if flops else 1, transcendentals=0
        ),
        name=name,
    )(*args)
    return result[0] if len(shapes) == 1 else result


def body(
    src_emb, src_state, dst_emb, dst_state, relations, src_index, dst_index, rel_index, neg_index
):
    wide, narrow = lax.axis_size("wide"), lax.axis_size("narrow")

    def moved(value, along=0, to=0, copies=False):
        pairs = []
        for w in range(wide):
            target = (w + along) % wide
            other_half = copies and w // (wide // 2) != target // (wide // 2)
            turn = to ^ 2 if other_half else to
            pairs += [(w * narrow + n, target * narrow + (n ^ turn)) for n in range(narrow)]
        return lax.ppermute(value, ("wide", "narrow"), pairs)

    rows, depth = dst_emb.shape
    edges = src_emb.shape[0]
    half = rows // 2
    src_index, dst_index, rel_index, neg_index = (
        a[0] for a in (src_index, dst_index, rel_index, neg_index)
    )
    negatives = neg_index.shape[1]
    dst, src, rel = dst_emb.T, src_emb.T, relations.T
    tall = depth + META

    here = lax.rem(lax.axis_index("narrow"), 2)
    payload = lax.dynamic_slice(dst, (0, here * half), (depth, half)).astype(BF)
    own = moved(payload, along=1, copies=True)
    edges_index = jnp.concatenate([src_index, dst_index, rel_index], axis=0)
    edges_index, payload = lax.optimization_barrier((edges_index, payload))

    src_state = src_state.reshape(1, edges)
    blocks = rows // LANES
    matmul = 2 * edges * rows * depth
    table = 2 * edges * relations.shape[0] * depth
    query, rel0 = call(
        query0_kernel,
        [((tall, edges), BF), ((depth, edges), BF)],
        [rel, src, edges_index],
        "query_step0",
        flops=table,
        limit=32,
    )
    query_c, query_y = moved(query, to=1), moved(query, to=2)
    query, dst_state = lax.optimization_barrier((query, dst_state))
    state = moved(dst_state.reshape(1, rows), along=1, copies=True)
    (
        query_t, target_at, rel1, count0, column, counts_sent, count1,
        src, src_state, src_index, dst_index,
    ) = call(
        functools.partial(prep_kernel, rows),
        [
            ((edges, depth), BF),
            ((edges, LANES), I32),
            ((depth, edges), BF),
            ((1, rows), F32),
            ((LANES, blocks), F32),
            ((2 * blocks, LANES), F32),
            ((1, rows), F32),
            (src.shape, F32),
            (src_state.shape, F32),
            (src_index.shape, I32),
            (dst_index.shape, I32),
        ],
        [rel, query, rel_index, neg_index, src, src_state, src_index, dst_index],
        "prepare",
        flops=table,
        limit=32,
    )
    own, query_c, rel1, state = lax.optimization_barrier((own, query_c, rel1, state))
    other = [moved(own[:, k : k + half // 2], to=1) for k in (0, half // 2)]

    query1, src1, src_state1 = call(
        functools.partial(src0_kernel, negatives),
        [((tall, edges), BF), ((depth, edges), F32), ((1, edges), F32)],
        [
            own, *other, query_t, target_at, count0, src, src_state,
            rel0, rel1, src_index, dst_index, counts_sent,
        ],
        "source_step0",
        limit=24,
    )
    next_own, next_y = moved(query1, along=-1), moved(query1, along=-1, to=2)
    query_y, query1 = lax.optimization_barrier((query_y, query1))
    query_cy = moved(query_y, to=1)

    block1, turned1, delta0, dst_state1 = call(
        functools.partial(dst0_kernel, negatives),
        [((depth, half), BF), ((half, depth), BF), ((depth, half), F32), ((1, half), F32)],
        [own, state, query, query_y, query_c, query_cy, column],
        "destination_step0",
        limit=24,
    )
    block1_own = moved(block1, along=1, copies=True)
    next_c = moved(next_own, to=1)

    first = call(
        functools.partial(dst1_first_kernel, negatives),
        [((depth, half), F32)],
        [turned1, next_own, next_c],
        "destination_step1_first",
        limit=24,
    )
    next_cy = moved(next_y, to=1)
    delta = call(
        functools.partial(dst1_kernel, negatives),
        [((tall, half), BF)],
        [turned1, first, next_own, next_y, next_cy, delta0, dst_state1],
        "destination_step1",
        flops=2 * matmul,
        limit=24,
    )
    home_own = moved(delta, along=-1, copies=True)

    block1_own, delta = lax.optimization_barrier((block1_own, delta))
    block1_other = [moved(block1_own[:, k : k + half // 2], to=1) for k in (0, half // 2)]
    src_out = call(
        functools.partial(src1_kernel, negatives),
        [((depth, edges), F32)],
        [block1_own, *block1_other, query1, count1, src1, src_state1, rel1, src_index],
        "source_step1",
        limit=24,
    )
    home_own, src_out = lax.optimization_barrier((home_own, src_out))
    home_other = moved(home_own, to=1)
    dst_out = ()
    for mine, home in ((True, home_own), (False, home_other)):
        dst_out = (
            call(
                functools.partial(final_kernel, mine),
                [((depth, rows), F32)],
                [dst, home, *dst_out],
                "destination_out",
                scratch=[pltpu.VMEM((depth, half), F32), pltpu.SemaphoreType.DMA((2,))],
                hbm=(2,),
                limit=16,
                out=0 if mine else 2,
            ),
        )
    dst_out = dst_out[0]
    return src_out.T, dst_out.T


def solution(mesh):
    in_specs = (
        P(("wide", "narrow"), None),
        P(("wide", "narrow")),
        P("wide", None),
        P("wide"),
        P(),
        P(("wide", "narrow"), None, None),
        P(("wide", "narrow"), None, None),
        P(("wide", "narrow"), None, None),
        P("wide", None, None),
    )
    out_specs = (P(("wide", "narrow"), None), P("wide", None))
    return jax.shard_map(body, mesh=mesh, in_specs=in_specs, out_specs=out_specs, check_vma=False)
```

```python
import functools

import jax
import jax.numpy as jnp
from jax import lax
from jax.experimental import pallas as pl
from jax.experimental.pallas import tpu as pltpu
from jax.sharding import PartitionSpec as P

LEARNING_RATE = 0.1
BF = jnp.bfloat16
F32 = jnp.float32
I32 = jnp.int32
META = 16
FINE = 32
LANES = 128
ROW_CUTS = 0, 144, 272
PIECE = 1920


def dot(a, b):
    return lax.dot_general(a, b, (((1,), (0,)), ((), ())), preferred_element_type=F32)


def dot_nt(a, b):
    return lax.dot_general(a, b, (((1,), (1,)), ((), ())), preferred_element_type=F32)


def core():
    return lax.rem(lax.axis_index("narrow"), 2)


def iota(shape, dim):
    return lax.broadcasted_iota(I32, shape, dim)


def one_hot(rows, index):
    return (iota((rows, index.shape[1]), 0) == index).astype(F32).astype(BF)


def eye(n):
    return (iota((n, n), 0) == iota((n, n), 1)).astype(F32).astype(BF)


def index_rows(index):
    fine = lax.rem(index, FINE)
    coarse = lax.div(index, FINE)
    at = iota((META, index.shape[1]), 0)
    parts = jnp.where(at == 0, coarse, jnp.where(at == 1, fine, 0))
    return parts.astype(F32).astype(BF)


def split(value):
    high = value.astype(BF)
    return high, (value - high.astype(F32)).astype(BF)


def picked(value, hot):
    high, low = split(value)
    return dot(high, hot) + dot(low, hot)


def summed(value, hot):
    high, low = split(value)
    return dot_nt(high, hot) + dot_nt(low, hot)


def coefficients(scores, count, is_target, negatives):
    tanh = jnp.tanh(0.5 * scores)
    scale = count * (0.5 / negatives)
    pull = jnp.where(is_target, 0.5 * tanh - 0.5, 0.0)
    return (scale * tanh + scale + pull).astype(BF)


def step_size(state, gradient):
    state = state + jnp.mean(gradient * gradient, axis=0, keepdims=True)
    return state, LEARNING_RATE / jnp.sqrt(state)


def count_grid(index, blocks):
    return one_hot(blocks, lax.div(index, LANES)), one_hot(LANES, lax.rem(index, LANES))


def relation_rows(rel_ref, index):
    depth, relations = rel_ref.shape
    block = lax.div(index, LANES)
    within = one_hot(LANES, lax.rem(index, LANES))
    found = jnp.zeros((depth, index.shape[1]), F32)
    for start in range(0, relations, PIECE):
        size = min(PIECE, relations - start)
        hot = jnp.concatenate(
            [
                within * (block == start // LANES + i).astype(F32).astype(BF)
                for i in range(size // LANES)
            ],
            axis=0,
        )
        found = found + dot(rel_ref[:, start : start + size], hot)
    return found


def lane_row(counts, out_ref):
    for i in range(counts.shape[0]):
        out_ref[:, i * LANES : (i + 1) * LANES] = counts[i : i + 1, :]


def query0_kernel(
    rel_ref, src_ref, index, q_ref, rel_out
):
    depth, edges = src_ref.shape
    src_index, dst_index, rel_index = index[0:1, :], index[2:3, :], index[4:5, :]
    found = relation_rows(rel_ref, rel_index)
    rel_out[...] = found.astype(BF)
    rows = picked(src_ref[...], one_hot(edges, src_index))
    q_ref[:depth, :] = (rows * found).astype(BF)
    q_ref[depth:, :] = index_rows(dst_index)


def prep_kernel(
    rows, rel_ref, q_ref, rel_index, neg_index, src_ref, state_ref, src_index, dst_index,
    qt_ref, at_ref, rel_out, count_ref, column_ref, next_ref, next_count_ref,
    src_out, state_out, src_index_out, dst_index_out,
):
    depth, edges = rel_out.shape
    src_out[...] = src_ref[...]
    state_out[...] = state_ref[...]
    src_index_out[...] = src_index[...]
    dst_index_out[...] = dst_index[...]
    blocks = rows // LANES
    flip = core() * (rows // 2)
    coarse, fine = count_grid(neg_index[0:1, :] ^ flip, blocks)
    lane_row(dot_nt(coarse, fine), count_ref)
    column_ref[...] = dot_nt(fine, coarse)
    coarse, fine = count_grid(neg_index[1:2, :] ^ flip, blocks)
    counts = dot_nt(coarse, fine)
    high = jnp.floor(counts * (1.0 / FINE))
    next_ref[...] = jnp.concatenate([high, counts - high * FINE], axis=0)
    lane_row(counts, next_count_ref)
    rel_out[...] = relation_rows(rel_ref, rel_index[1:2, :]).astype(BF)
    query_t, target_at = turned_query(q_ref, depth, flip)
    qt_ref[...] = query_t
    at_ref[...] = jnp.broadcast_to(target_at, at_ref.shape)


def turned_query(q_ref, depth, flip):
    turn = eye(q_ref.shape[1])
    parts = dot_nt(turn, q_ref[depth:, :])
    target_at = (parts[:, 0:1] * FINE + parts[:, 1:2]).astype(I32) ^ flip
    return dot_nt(turn, q_ref[:depth, :]).astype(BF), target_at


def query_gradient(negatives, blocks, query_t, target_at, count_ref):
    total = 0.0
    start = 0
    for block in blocks:
        rows = block.shape[1]
        scores = dot(query_t, block)
        target = iota(scores.shape, 1) + start == target_at
        count = count_ref[:, start : start + rows]
        total += dot_nt(block, coefficients(scores, count, target, negatives))
        start += rows
    return total


def src0_first_kernel(negatives, own_ref, qt_ref, at_ref, count_ref, grad_out):
    half = own_ref.shape[1]
    grad_out[...] = query_gradient(
        negatives, [own_ref[...]], qt_ref[...], at_ref[:, 0:1], count_ref[:, :half]
    )


def src0_kernel(
    negatives, first_ref, other_a, other_b, qt_ref, at_ref, count_ref, src_ref, state_ref,
    rel0_ref, rel1_ref, src_index, dst_index, next_ref, q_ref, src_out, state_out,
):
    depth, edges = src_ref.shape
    block = jnp.concatenate([other_a[...], other_b[...]], axis=1)
    half = block.shape[1]
    grad = first_ref[...] + query_gradient(
        negatives, [block], qt_ref[...], at_ref[:, 0:1] - half, count_ref[:, half:]
    )
    gradient = summed(grad * rel0_ref[...].astype(F32), one_hot(edges, src_index[0:1, :]))
    state, size = step_size(state_ref[...], gradient)
    src = src_ref[...] - gradient * size
    src_out[...] = src
    state_out[...] = state
    rows = picked(src, one_hot(edges, src_index[1:2, :]))
    q_ref[:depth, :] = (rows * rel1_ref[...].astype(F32)).astype(BF)
    blocks = next_ref.shape[0] // 2
    counts = jnp.concatenate([next_ref[:blocks, :], next_ref[blocks:, :]], axis=1)
    gap = jnp.zeros((META // 2, edges), F32)
    meta = index_rows(dst_index[1:2, :]).astype(F32)
    q_ref[depth:, :] = (meta + jnp.concatenate([gap, counts], axis=0)).astype(BF)


def src1_kernel(
    negatives, own_ref, other_a, other_b, other_c, q_ref, count_ref, src_ref, state_ref, rel_ref,
    src_index, src_out,
):
    depth, edges = src_ref.shape
    half = own_ref.shape[1]
    query_t, target_at = turned_query(q_ref, depth, core() * half)
    blocks = own_ref[...], jnp.concatenate([other_a[...], other_b[...], other_c[...]], axis=0)
    grad = query_gradient(negatives, blocks, query_t, target_at, count_ref)
    gradient = summed(grad * rel_ref[...].astype(F32), one_hot(edges, src_index[1:2, :]))
    _, size = step_size(state_ref[...], gradient)
    src_out[...] = src_ref[...] - gradient * size


def targets(q_ref, depth, flip):
    parts = q_ref[depth:, :].astype(F32)
    return (parts[0:1, :] * FINE + parts[1:2, :]).astype(I32) ^ flip


def sent_counts(q_ref, depth):
    parts = dot_nt(eye(LANES), q_ref[depth:, :LANES]) * FINE
    parts = parts + dot_nt(eye(LANES), q_ref[depth:, LANES : 2 * LANES])
    return parts[:, META // 2 :]


def row_coefficients(block_t, start, q_ref, column, flip, negatives):
    rows, depth = block_t.shape
    scores = dot(block_t, q_ref[:depth, :])
    target = iota(scores.shape, 0) + start == targets(q_ref, depth, flip)
    first = start // LANES
    count = jnp.concatenate(
        [column[:, first + i : first + i + 1] for i in range(rows // LANES)], axis=0
    )
    return coefficients(scores, count, target, negatives)


def dst_gradient(block_t, q_refs, column, flip, negatives, start=0):
    rows, depth = block_t.shape
    total = jnp.zeros((depth, rows), F32)
    for q_ref in q_refs:
        weights = row_coefficients(block_t, start, q_ref, column, flip, negatives)
        total += dot_nt(q_ref[:depth, :], weights)
    return total


def turned(block):
    step = 2 * LANES
    turn = eye(step)
    return jnp.concatenate(
        [dot_nt(turn, block[:, k : k + step]).astype(BF) for k in range(0, block.shape[1], step)],
        axis=0,
    )


def dst0_kernel(
    negatives, own_ref, old_ref, qa, qb, qc, qd, column_ref,
    block_out, turned_out, delta_out, state_out,
):
    depth, half = delta_out.shape
    block = own_ref[...]
    columns = pl.ds(pl.multiple_of(core() * half, half), half)
    queries = qa, qb, qc, qd
    gradient = dst_gradient(
        turned(block), queries, column_ref[...], core() * half, negatives
    )
    state, size = step_size(old_ref[:, columns], gradient)
    delta = gradient * size
    block = (block.astype(F32) - delta).astype(BF)
    block_out[...] = block
    turned_out[...] = turned(block)
    delta_out[...] = delta
    state_out[...] = state


def dst1_first_kernel(negatives, turned_ref, qa, qb, qc, grad_out):
    depth, half = grad_out.shape
    grad_out[...] = dst_gradient(
        turned_ref[...], (qa, qb, qc), sent_counts(qa, depth), core() * half, negatives
    )


def dst1_kernel(
    negatives, start, turned_ref, first_ref, qa, qd, delta_ref, state_ref, *refs
):
    delta_out = refs[-1]
    depth, half = delta_ref.shape
    part = slice(start, start + delta_out.shape[1])
    gradient = first_ref[:, part] + dst_gradient(
        turned_ref[part, :], (qd,), sent_counts(qa, depth), core() * half, negatives, start
    )
    _, size = step_size(state_ref[:, part], gradient)
    delta_out[...] = (delta_ref[:, part] + gradient * size).astype(BF)


def final_kernel(start, parts, emb_ref, own_ref, *refs):
    out_ref, held, sems = refs[-3:]
    size = own_ref.shape[1]
    other = jnp.concatenate([ref[...] for ref in refs[:parts]], axis=1)
    half = emb_ref.shape[1] // 2
    here = core()
    copies = []
    for i, (place, delta) in enumerate(((here, own_ref[...]), (1 - here, other))):
        columns = pl.ds(pl.multiple_of(place * half + start, size), size)
        held[i] = emb_ref[:, columns] - delta.astype(F32)
        copies.append(pltpu.make_async_copy(held.at[i], out_ref.at[:, columns], sems.at[i]))
        copies[-1].start()
    for copy in copies:
        copy.wait()


def call(kernel, outs, args, name, flops=None, scratch=(), hbm=(), limit=32, out=None):
    vmem = pl.BlockSpec(memory_space=pltpu.VMEM)
    anywhere = pl.BlockSpec(memory_space=pltpu.HBM)
    shapes = [jax.ShapeDtypeStruct(shape, dtype) for shape, dtype in outs]
    size = sum(a.size * a.dtype.itemsize for a in [*args, *shapes])
    result = pl.pallas_call(
        kernel,
        out_shape=shapes,
        in_specs=[anywhere if i in hbm else vmem for i in range(len(args))],
        out_specs=[vmem if out is None else anywhere] * len(shapes),
        input_output_aliases={out: 0} if out else {},
        scratch_shapes=list(scratch),
        compiler_params=pltpu.CompilerParams(vmem_limit_bytes=int(limit * 2**20)),
        cost_estimate=pl.CostEstimate(
            flops=flops or 1, bytes_accessed=size if flops else 1, transcendentals=0
        ),
        name=name,
    )(*args)
    return result[0] if len(shapes) == 1 else result


def body(
    src_emb, src_state, dst_emb, dst_state, relations, src_index, dst_index, rel_index, neg_index
):
    wide, narrow = lax.axis_size("wide"), lax.axis_size("narrow")

    def moved(value, along=0, to=0, copies=False):
        pairs = []
        for w in range(wide):
            target = (w + along) % wide
            other_half = copies and w // (wide // 2) != target // (wide // 2)
            turn = to ^ 2 if other_half else to
            pairs += [(w * narrow + n, target * narrow + (n ^ turn)) for n in range(narrow)]
        return lax.ppermute(value, ("wide", "narrow"), pairs)

    rows, depth = dst_emb.shape
    edges = src_emb.shape[0]
    half = rows // 2
    src_index, dst_index, rel_index, neg_index = (
        a[0] for a in (src_index, dst_index, rel_index, neg_index)
    )
    negatives = neg_index.shape[1]
    dst, src, rel = dst_emb.T, src_emb.T, relations.T
    tall = depth + META

    here = lax.rem(lax.axis_index("narrow"), 2)
    payload = lax.dynamic_slice(dst, (0, here * half), (depth, half)).astype(BF)
    own = moved(payload, along=1, copies=True)
    edges_index = jnp.concatenate([src_index, dst_index, rel_index], axis=0)
    edges_index, payload = lax.optimization_barrier((edges_index, payload))

    src_state = src_state.reshape(1, edges)
    blocks = rows // LANES
    matmul = 2 * edges * rows * depth
    table = 2 * edges * relations.shape[0] * depth
    query, rel0 = call(
        query0_kernel,
        [((tall, edges), BF), ((depth, edges), BF)],
        [rel, src, edges_index],
        "query_step0",
        flops=table,
        limit=32,
    )
    query_c, query_y = moved(query, to=1), moved(query, to=2)
    query, dst_state = lax.optimization_barrier((query, dst_state))
    state = moved(dst_state.reshape(1, rows), along=1, copies=True)
    (
        query_t, target_at, rel1, count0, column, counts_sent, count1,
        src, src_state, src_index, dst_index,
    ) = call(
        functools.partial(prep_kernel, rows),
        [
            ((edges, depth), BF),
            ((edges, LANES), I32),
            ((depth, edges), BF),
            ((1, rows), F32),
            ((LANES, blocks), F32),
            ((2 * blocks, LANES), F32),
            ((1, rows), F32),
            (src.shape, F32),
            (src_state.shape, F32),
            (src_index.shape, I32),
            (dst_index.shape, I32),
        ],
        [rel, query, rel_index, neg_index, src, src_state, src_index, dst_index],
        "prepare",
        flops=table,
        limit=32,
    )
    own, query_c, rel1, state = lax.optimization_barrier((own, query_c, rel1, state))
    other = [moved(own[:, k : k + half // 2], to=1) for k in (0, half // 2)]

    first = call(
        functools.partial(src0_first_kernel, negatives),
        [((depth, edges), F32)],
        [own, query_t, target_at, count0],
        "source_step0_first",
        limit=24,
    )
    query1, src1, src_state1 = call(
        functools.partial(src0_kernel, negatives),
        [((tall, edges), BF), ((depth, edges), F32), ((1, edges), F32)],
        [
            first, *other, query_t, target_at, count0, src, src_state,
            rel0, rel1, src_index, dst_index, counts_sent,
        ],
        "source_step0",
        limit=24,
    )
    next_own, next_y = moved(query1, along=-1), moved(query1, along=-1, to=2)
    query_y, query1 = lax.optimization_barrier((query_y, query1))
    query_cy = moved(query_y, to=1)

    block1, turned1, delta0, dst_state1 = call(
        functools.partial(dst0_kernel, negatives),
        [((depth, half), BF), ((half, depth), BF), ((depth, half), F32), ((1, half), F32)],
        [own, state, query, query_y, query_c, query_cy, column],
        "destination_step0",
        limit=24,
    )
    block1_own = moved(block1, along=1, copies=True)
    next_c = moved(next_own, to=1)

    first = call(
        functools.partial(dst1_first_kernel, negatives),
        [((depth, half), F32)],
        [turned1, next_own, next_c, next_y],
        "destination_step1_first",
        limit=24,
    )
    next_cy = moved(next_y, to=1)
    piece = half // 2
    deltas = []
    for start in range(0, half, piece):
        deltas.append(
            call(
                functools.partial(dst1_kernel, negatives, start),
                [((depth, piece), BF)],
                [turned1, first, next_own, next_cy, delta0, dst_state1, *deltas],
                "destination_step1",
                limit=24,
            )
        )
    homes = [moved(delta, along=-1, copies=True) for delta in deltas]

    block1_own, *_ = lax.optimization_barrier((block1_own, *deltas))
    block1_other = [
        moved(block1_own[a:b], to=1) for a, b in zip(ROW_CUTS, (*ROW_CUTS[1:], depth))
    ]
    src_out = call(
        functools.partial(src1_kernel, negatives),
        [((depth, edges), F32)],
        [block1_own, *block1_other, query1, count1, src1, src_state1, rel1, src_index],
        "source_step1",
        limit=24,
    )
    homes[0], src_out = lax.optimization_barrier((homes[0], src_out))
    def exchanged(home, parts):
        size = piece // parts
        return [moved(home[:, k * size : (k + 1) * size], to=1) for k in range(parts)]

    dst_out = ()
    for i, home in enumerate(homes):
        if i:
            home, *dst_out = lax.optimization_barrier((home, *dst_out))
        dst_out = (
            call(
                functools.partial(final_kernel, i * piece, 2 - i),
                [((depth, rows), F32)],
                [dst, home, *exchanged(home, 2 - i), *dst_out],
                "destination_out",
                flops=i * matmul // 4,
                scratch=[pltpu.VMEM((2, depth, piece), F32), pltpu.SemaphoreType.DMA((2,))],
                hbm=(3,) if i else (),
                limit=16,
                out=3 * i,
            ),
        )
    dst_out = dst_out[0]
    return src_out.T, dst_out.T


def solution(mesh):
    in_specs = (
        P(("wide", "narrow"), None),
        P(("wide", "narrow")),
        P("wide", None),
        P("wide"),
        P(),
        P(("wide", "narrow"), None, None),
        P(("wide", "narrow"), None, None),
        P(("wide", "narrow"), None, None),
        P("wide", None, None),
    )
    out_specs = (P(("wide", "narrow"), None), P("wide", None))
    return jax.shard_map(body, mesh=mesh, in_specs=in_specs, out_specs=out_specs, check_vma=False)
```

```python
import functools

import jax
import jax.numpy as jnp
from jax import lax
from jax.experimental import pallas as pl
from jax.experimental.pallas import tpu as pltpu
from jax.sharding import PartitionSpec as P

LEARNING_RATE = 0.1
BF = jnp.bfloat16
F32 = jnp.float32
I32 = jnp.int32
META = 16
FINE = 32
LANES = 128
ROW_CUTS = 0, 144, 272
PIECE = 1920


def dot(a, b):
    return lax.dot_general(a, b, (((1,), (0,)), ((), ())), preferred_element_type=F32)


def dot_nt(a, b):
    return lax.dot_general(a, b, (((1,), (1,)), ((), ())), preferred_element_type=F32)


def core():
    return lax.rem(lax.axis_index("narrow"), 2)


def iota(shape, dim):
    return lax.broadcasted_iota(I32, shape, dim)


def one_hot(rows, index):
    return (iota((rows, index.shape[1]), 0) == index).astype(F32).astype(BF)


def eye(n):
    return (iota((n, n), 0) == iota((n, n), 1)).astype(F32).astype(BF)


def index_rows(index):
    fine = lax.rem(index, FINE)
    coarse = lax.div(index, FINE)
    at = iota((META, index.shape[1]), 0)
    parts = jnp.where(at == 0, coarse, jnp.where(at == 1, fine, 0))
    return parts.astype(F32).astype(BF)


def split(value):
    high = value.astype(BF)
    return high, (value - high.astype(F32)).astype(BF)


def picked(value, hot):
    high, low = split(value)
    return dot(high, hot) + dot(low, hot)


def summed(value, hot):
    high, low = split(value)
    return dot_nt(high, hot) + dot_nt(low, hot)


def coefficients(scores, count, is_target, negatives):
    tanh = jnp.tanh(0.5 * scores)
    scale = count * (0.5 / negatives)
    pull = jnp.where(is_target, 0.5 * tanh - 0.5, 0.0)
    return (scale * tanh + scale + pull).astype(BF)


def step_size(state, gradient):
    state = state + jnp.mean(gradient * gradient, axis=0, keepdims=True)
    return state, LEARNING_RATE / jnp.sqrt(state)


def count_grid(index, blocks):
    return one_hot(blocks, lax.div(index, LANES)), one_hot(LANES, lax.rem(index, LANES))


def relation_rows(rel_ref, index):
    depth, relations = rel_ref.shape
    block = lax.div(index, LANES)
    within = one_hot(LANES, lax.rem(index, LANES))
    found = jnp.zeros((depth, index.shape[1]), F32)
    for start in range(0, relations, PIECE):
        size = min(PIECE, relations - start)
        hot = jnp.concatenate(
            [
                within * (block == start // LANES + i).astype(F32).astype(BF)
                for i in range(size // LANES)
            ],
            axis=0,
        )
        found = found + dot(rel_ref[:, start : start + size], hot)
    return found


def lane_row(counts, out_ref):
    for i in range(counts.shape[0]):
        out_ref[:, i * LANES : (i + 1) * LANES] = counts[i : i + 1, :]


def query0_kernel(
    rel_ref, src_ref, index, q_ref, rel_out
):
    depth, edges = src_ref.shape
    src_index, dst_index, rel_index = index[0:1, :], index[2:3, :], index[4:5, :]
    found = relation_rows(rel_ref, rel_index)
    rel_out[...] = found.astype(BF)
    rows = picked(src_ref[...], one_hot(edges, src_index))
    q_ref[:depth, :] = (rows * found).astype(BF)
    q_ref[depth:, :] = index_rows(dst_index)


def prep_kernel(
    rows, rel_ref, q_ref, rel_index, neg_index, src_ref, state_ref, src_index, dst_index,
    qt_ref, at_ref, rel_out, count_ref, column_ref, next_ref, next_count_ref,
    src_out, state_out, src_index_out, dst_index_out,
):
    depth, edges = rel_out.shape
    src_out[...] = src_ref[...]
    state_out[...] = state_ref[...]
    src_index_out[...] = src_index[...]
    dst_index_out[...] = dst_index[...]
    blocks = rows // LANES
    flip = core() * (rows // 2)
    coarse, fine = count_grid(neg_index[0:1, :] ^ flip, blocks)
    lane_row(dot_nt(coarse, fine), count_ref)
    column_ref[...] = dot_nt(fine, coarse)
    coarse, fine = count_grid(neg_index[1:2, :] ^ flip, blocks)
    counts = dot_nt(coarse, fine)
    high = jnp.floor(counts * (1.0 / FINE))
    next_ref[...] = jnp.concatenate([high, counts - high * FINE], axis=0)
    lane_row(counts, next_count_ref)
    rel_out[...] = relation_rows(rel_ref, rel_index[1:2, :]).astype(BF)
    query_t, target_at = turned_query(q_ref, depth, flip)
    qt_ref[...] = query_t
    at_ref[...] = jnp.broadcast_to(target_at, at_ref.shape)


def turned_query(q_ref, depth, flip):
    turn = eye(q_ref.shape[1])
    parts = dot_nt(turn, q_ref[depth:, :])
    target_at = (parts[:, 0:1] * FINE + parts[:, 1:2]).astype(I32) ^ flip
    return dot_nt(turn, q_ref[:depth, :]).astype(BF), target_at


def query_gradient(negatives, blocks, query_t, target_at, count_ref):
    total = 0.0
    start = 0
    for block in blocks:
        rows = block.shape[1]
        scores = dot(query_t, block)
        target = iota(scores.shape, 1) + start == target_at
        count = count_ref[:, start : start + rows]
        total += dot_nt(block, coefficients(scores, count, target, negatives))
        start += rows
    return total


def src0_first_kernel(negatives, own_ref, qt_ref, at_ref, count_ref, grad_out):
    half = own_ref.shape[1]
    grad_out[...] = query_gradient(
        negatives, [own_ref[...]], qt_ref[...], at_ref[:, 0:1], count_ref[:, :half]
    )


def src0_kernel(
    negatives, first_ref, other_a, other_b, qt_ref, at_ref, count_ref, src_ref, state_ref,
    rel0_ref, rel1_ref, src_index, dst_index, next_ref, q_ref, src_out, state_out,
):
    depth, edges = src_ref.shape
    block = jnp.concatenate([other_a[...], other_b[...]], axis=1)
    half = block.shape[1]
    grad = first_ref[...] + query_gradient(
        negatives, [block], qt_ref[...], at_ref[:, 0:1] - half, count_ref[:, half:]
    )
    gradient = summed(grad * rel0_ref[...].astype(F32), one_hot(edges, src_index[0:1, :]))
    state, size = step_size(state_ref[...], gradient)
    src = src_ref[...] - gradient * size
    src_out[...] = src
    state_out[...] = state
    rows = picked(src, one_hot(edges, src_index[1:2, :]))
    q_ref[:depth, :] = (rows * rel1_ref[...].astype(F32)).astype(BF)
    blocks = next_ref.shape[0] // 2
    counts = jnp.concatenate([next_ref[:blocks, :], next_ref[blocks:, :]], axis=1)
    gap = jnp.zeros((META // 2, edges), F32)
    meta = index_rows(dst_index[1:2, :]).astype(F32)
    q_ref[depth:, :] = (meta + jnp.concatenate([gap, counts], axis=0)).astype(BF)


def src1_kernel(
    negatives, own_ref, other_a, other_b, other_c, q_ref, count_ref, src_ref, state_ref, rel_ref,
    src_index, src_out,
):
    depth, edges = src_ref.shape
    half = own_ref.shape[1]
    query_t, target_at = turned_query(q_ref, depth, core() * half)
    blocks = own_ref[...], jnp.concatenate([other_a[...], other_b[...], other_c[...]], axis=0)
    grad = query_gradient(negatives, blocks, query_t, target_at, count_ref)
    gradient = summed(grad * rel_ref[...].astype(F32), one_hot(edges, src_index[1:2, :]))
    _, size = step_size(state_ref[...], gradient)
    src_out[...] = src_ref[...] - gradient * size


def targets(q_ref, depth, flip):
    parts = q_ref[depth:, :].astype(F32)
    return (parts[0:1, :] * FINE + parts[1:2, :]).astype(I32) ^ flip


def sent_counts(q_ref, depth):
    parts = dot_nt(eye(LANES), q_ref[depth:, :LANES]) * FINE
    parts = parts + dot_nt(eye(LANES), q_ref[depth:, LANES : 2 * LANES])
    return parts[:, META // 2 :]


def row_coefficients(block_t, start, q_ref, column, flip, negatives):
    rows, depth = block_t.shape
    scores = dot(block_t, q_ref[:depth, :])
    target = iota(scores.shape, 0) + start == targets(q_ref, depth, flip)
    first = start // LANES
    count = jnp.concatenate(
        [column[:, first + i : first + i + 1] for i in range(rows // LANES)], axis=0
    )
    return coefficients(scores, count, target, negatives)


def dst_gradient(block_t, q_refs, column, flip, negatives, start=0):
    rows, depth = block_t.shape
    total = jnp.zeros((depth, rows), F32)
    for q_ref in q_refs:
        weights = row_coefficients(block_t, start, q_ref, column, flip, negatives)
        total += dot_nt(q_ref[:depth, :], weights)
    return total


def turned(block):
    step = 2 * LANES
    turn = eye(step)
    return jnp.concatenate(
        [dot_nt(turn, block[:, k : k + step]).astype(BF) for k in range(0, block.shape[1], step)],
        axis=0,
    )


def dst0_kernel(
    negatives, own_ref, old_ref, qa, qb, qc, qd, column_ref,
    block_out, turned_out, delta_out, state_out,
):
    depth, half = delta_out.shape
    block = own_ref[...]
    columns = pl.ds(pl.multiple_of(core() * half, half), half)
    queries = qa, qb, qc, qd
    gradient = dst_gradient(
        turned(block), queries, column_ref[...], core() * half, negatives
    )
    state, size = step_size(old_ref[:, columns], gradient)
    delta = gradient * size
    block = (block.astype(F32) - delta).astype(BF)
    block_out[...] = block
    turned_out[...] = turned(block)
    delta_out[...] = delta
    state_out[...] = state


def dst1_first_kernel(negatives, turned_ref, qa, qb, qc, grad_out):
    depth, half = grad_out.shape
    grad_out[...] = dst_gradient(
        turned_ref[...], (qa, qb, qc), sent_counts(qa, depth), core() * half, negatives
    )


def dst1_kernel(
    negatives, start, turned_ref, first_ref, qa, qd, delta_ref, state_ref, *refs
):
    delta_out = refs[-1]
    depth, half = delta_ref.shape
    part = slice(start, start + delta_out.shape[1])
    gradient = first_ref[:, part] + dst_gradient(
        turned_ref[part, :], (qd,), sent_counts(qa, depth), core() * half, negatives, start
    )
    _, size = step_size(state_ref[:, part], gradient)
    delta_out[...] = (delta_ref[:, part] + gradient * size).astype(BF)


def final_kernel(start, sides, emb_ref, *refs):
    out_ref, held, sems = refs[-3:]
    half = emb_ref.shape[1] // 2
    copies = []
    for i, (side, count) in enumerate(sides):
        delta = jnp.concatenate([ref[...] for ref in refs[:count]], axis=1)
        refs = refs[count:]
        size = delta.shape[1]
        place = core() if side == 0 else 1 - core()
        columns = pl.ds(pl.multiple_of(place * half + start, size), size)
        held[i] = emb_ref[:, columns] - delta.astype(F32)
        copies.append(pltpu.make_async_copy(held.at[i], out_ref.at[:, columns], sems.at[i]))
        copies[-1].start()
    for copy in copies:
        copy.wait()


def call(kernel, outs, args, name, flops=None, scratch=(), hbm=(), limit=32, out=None):
    vmem = pl.BlockSpec(memory_space=pltpu.VMEM)
    anywhere = pl.BlockSpec(memory_space=pltpu.HBM)
    shapes = [jax.ShapeDtypeStruct(shape, dtype) for shape, dtype in outs]
    size = sum(a.size * a.dtype.itemsize for a in [*args, *shapes])
    result = pl.pallas_call(
        kernel,
        out_shape=shapes,
        in_specs=[anywhere if i in hbm else vmem for i in range(len(args))],
        out_specs=[vmem if out is None else anywhere] * len(shapes),
        input_output_aliases={out: 0} if out else {},
        scratch_shapes=list(scratch),
        compiler_params=pltpu.CompilerParams(vmem_limit_bytes=int(limit * 2**20)),
        cost_estimate=pl.CostEstimate(
            flops=flops or 1, bytes_accessed=size if flops else 1, transcendentals=0
        ),
        name=name,
    )(*args)
    return result[0] if len(shapes) == 1 else result


def body(
    src_emb, src_state, dst_emb, dst_state, relations, src_index, dst_index, rel_index, neg_index
):
    wide, narrow = lax.axis_size("wide"), lax.axis_size("narrow")

    def moved(value, along=0, to=0, copies=False):
        pairs = []
        for w in range(wide):
            target = (w + along) % wide
            other_half = copies and w // (wide // 2) != target // (wide // 2)
            turn = to ^ 2 if other_half else to
            pairs += [(w * narrow + n, target * narrow + (n ^ turn)) for n in range(narrow)]
        return lax.ppermute(value, ("wide", "narrow"), pairs)

    rows, depth = dst_emb.shape
    edges = src_emb.shape[0]
    half = rows // 2
    src_index, dst_index, rel_index, neg_index = (
        a[0] for a in (src_index, dst_index, rel_index, neg_index)
    )
    negatives = neg_index.shape[1]
    dst, src, rel = dst_emb.T, src_emb.T, relations.T
    tall = depth + META

    here = lax.rem(lax.axis_index("narrow"), 2)
    payload = lax.dynamic_slice(dst, (0, here * half), (depth, half)).astype(BF)
    own = moved(payload, along=1, copies=True)
    edges_index = jnp.concatenate([src_index, dst_index, rel_index], axis=0)
    edges_index, payload = lax.optimization_barrier((edges_index, payload))

    src_state = src_state.reshape(1, edges)
    blocks = rows // LANES
    matmul = 2 * edges * rows * depth
    table = 2 * edges * relations.shape[0] * depth
    query, rel0 = call(
        query0_kernel,
        [((tall, edges), BF), ((depth, edges), BF)],
        [rel, src, edges_index],
        "query_step0",
        flops=table,
        limit=32,
    )
    query_c, query_y = moved(query, to=1), moved(query, to=2)
    query, dst_state = lax.optimization_barrier((query, dst_state))
    state = moved(dst_state.reshape(1, rows), along=1, copies=True)
    (
        query_t, target_at, rel1, count0, column, counts_sent, count1,
        src, src_state, src_index, dst_index,
    ) = call(
        functools.partial(prep_kernel, rows),
        [
            ((edges, depth), BF),
            ((edges, LANES), I32),
            ((depth, edges), BF),
            ((1, rows), F32),
            ((LANES, blocks), F32),
            ((2 * blocks, LANES), F32),
            ((1, rows), F32),
            (src.shape, F32),
            (src_state.shape, F32),
            (src_index.shape, I32),
            (dst_index.shape, I32),
        ],
        [rel, query, rel_index, neg_index, src, src_state, src_index, dst_index],
        "prepare",
        flops=table,
        limit=32,
    )
    own, query_c, rel1, state = lax.optimization_barrier((own, query_c, rel1, state))
    other = [moved(own[:, k : k + half // 2], to=1) for k in (0, half // 2)]

    first = call(
        functools.partial(src0_first_kernel, negatives),
        [((depth, edges), F32)],
        [own, query_t, target_at, count0],
        "source_step0_first",
        limit=24,
    )
    query1, src1, src_state1 = call(
        functools.partial(src0_kernel, negatives),
        [((tall, edges), BF), ((depth, edges), F32), ((1, edges), F32)],
        [
            first, *other, query_t, target_at, count0, src, src_state,
            rel0, rel1, src_index, dst_index, counts_sent,
        ],
        "source_step0",
        limit=24,
    )
    next_own, next_y = moved(query1, along=-1), moved(query1, along=-1, to=2)
    query_y, query1 = lax.optimization_barrier((query_y, query1))
    query_cy = moved(query_y, to=1)

    block1, turned1, delta0, dst_state1 = call(
        functools.partial(dst0_kernel, negatives),
        [((depth, half), BF), ((half, depth), BF), ((depth, half), F32), ((1, half), F32)],
        [own, state, query, query_y, query_c, query_cy, column],
        "destination_step0",
        limit=24,
    )
    block1_own = moved(block1, along=1, copies=True)
    next_c = moved(next_own, to=1)

    first = call(
        functools.partial(dst1_first_kernel, negatives),
        [((depth, half), F32)],
        [turned1, next_own, next_c, next_y],
        "destination_step1_first",
        limit=24,
    )
    next_cy = moved(next_y, to=1)
    piece = half // 2
    deltas = []
    for start in range(0, half, piece):
        deltas.append(
            call(
                functools.partial(dst1_kernel, negatives, start),
                [((depth, piece), BF)],
                [turned1, first, next_own, next_cy, delta0, dst_state1, *deltas],
                "destination_step1",
                limit=24,
            )
        )
    homes = [moved(delta, along=-1, copies=True) for delta in deltas]

    block1_own, *_ = lax.optimization_barrier((block1_own, *deltas))
    block1_other = [
        moved(block1_own[a:b], to=1) for a, b in zip(ROW_CUTS, (*ROW_CUTS[1:], depth))
    ]
    src_out = call(
        functools.partial(src1_kernel, negatives),
        [((depth, edges), F32)],
        [block1_own, *block1_other, query1, count1, src1, src_state1, rel1, src_index],
        "source_step1",
        limit=24,
    )
    homes[0], src_out = lax.optimization_barrier((homes[0], src_out))
    def final(start, sides, changes, done):
        return call(
            functools.partial(final_kernel, start, sides),
            [((depth, rows), F32)],
            [dst, *changes, *done],
            "destination_out",
            scratch=[
                pltpu.VMEM((len(sides), depth, piece), F32),
                pltpu.SemaphoreType.DMA((len(sides),)),
            ],
            hbm=(1 + len(changes),),
            limit=16,
            out=1 + len(changes) if done else 0,
        )

    cuts = range(0, piece, LANES)
    other = [moved(homes[0][:, k : k + LANES], to=1) for k in cuts]
    dst_out = final(0, ((0, 1), (1, len(other))), [homes[0], *other], ())
    home, dst_out = lax.optimization_barrier((homes[1], dst_out))
    other = moved(home, to=1)
    dst_out = final(piece, ((0, 1),), [home], (dst_out,))
    dst_out = final(piece, ((1, 1),), [other], (dst_out,))
    return src_out.T, dst_out.T


def solution(mesh):
    in_specs = (
        P(("wide", "narrow"), None),
        P(("wide", "narrow")),
        P("wide", None),
        P("wide"),
        P(),
        P(("wide", "narrow"), None, None),
        P(("wide", "narrow"), None, None),
        P(("wide", "narrow"), None, None),
        P("wide", None, None),
    )
    out_specs = (P(("wide", "narrow"), None), P("wide", None))
    return jax.shard_map(body, mesh=mesh, in_specs=in_specs, out_specs=out_specs, check_vma=False)
```

```python
import functools

import jax
import jax.numpy as jnp
from jax import lax
from jax.experimental import pallas as pl
from jax.experimental.pallas import tpu as pltpu
from jax.sharding import PartitionSpec as P

LEARNING_RATE = 0.1
BF = jnp.bfloat16
F32 = jnp.float32
I32 = jnp.int32
META = 16
FINE = 32
LANES = 128
ROW_CUTS = 0, 144, 272
PIECE = 1920


def dot(a, b):
    return lax.dot_general(a, b, (((1,), (0,)), ((), ())), preferred_element_type=F32)


def dot_nt(a, b):
    return lax.dot_general(a, b, (((1,), (1,)), ((), ())), preferred_element_type=F32)


def core():
    return lax.rem(lax.axis_index("narrow"), 2)


def iota(shape, dim):
    return lax.broadcasted_iota(I32, shape, dim)


def one_hot(rows, index):
    return (iota((rows, index.shape[1]), 0) == index).astype(F32).astype(BF)


def eye(n):
    return (iota((n, n), 0) == iota((n, n), 1)).astype(F32).astype(BF)


def index_rows(index):
    fine = lax.rem(index, FINE)
    coarse = lax.div(index, FINE)
    at = iota((META, index.shape[1]), 0)
    parts = jnp.where(at == 0, coarse, jnp.where(at == 1, fine, 0))
    return parts.astype(F32).astype(BF)


def split(value):
    high = value.astype(BF)
    return high, (value - high.astype(F32)).astype(BF)


def picked(value, hot):
    high, low = split(value)
    return dot(high, hot) + dot(low, hot)


def summed(value, hot):
    high, low = split(value)
    return dot_nt(high, hot) + dot_nt(low, hot)


def coefficients(scores, count, is_target, negatives):
    tanh = jnp.tanh(0.5 * scores)
    scale = count * (0.5 / negatives)
    pull = jnp.where(is_target, 0.5 * tanh - 0.5, 0.0)
    return (scale * tanh + scale + pull).astype(BF)


def step_size(state, gradient):
    state = state + jnp.mean(gradient * gradient, axis=0, keepdims=True)
    return state, LEARNING_RATE / jnp.sqrt(state)


def count_grid(index, blocks):
    return one_hot(blocks, lax.div(index, LANES)), one_hot(LANES, lax.rem(index, LANES))


def relation_rows(rel_ref, index):
    depth, relations = rel_ref.shape
    block = lax.div(index, LANES)
    within = one_hot(LANES, lax.rem(index, LANES))
    found = jnp.zeros((depth, index.shape[1]), F32)
    for start in range(0, relations, PIECE):
        size = min(PIECE, relations - start)
        hot = jnp.concatenate(
            [
                within * (block == start // LANES + i).astype(F32).astype(BF)
                for i in range(size // LANES)
            ],
            axis=0,
        )
        found = found + dot(rel_ref[:, start : start + size], hot)
    return found


def lane_row(counts, out_ref):
    for i in range(counts.shape[0]):
        out_ref[:, i * LANES : (i + 1) * LANES] = counts[i : i + 1, :]


def query0_kernel(
    rel_ref, src_ref, index, q_ref, rel_out
):
    depth, edges = src_ref.shape
    src_index, dst_index, rel_index = index[0:1, :], index[2:3, :], index[4:5, :]
    found = relation_rows(rel_ref, rel_index)
    rel_out[...] = found.astype(BF)
    rows = picked(src_ref[...], one_hot(edges, src_index))
    q_ref[:depth, :] = (rows * found).astype(BF)
    q_ref[depth:, :] = index_rows(dst_index)


def prep_kernel(
    rows, rel_ref, q_ref, rel_index, neg_index, src_ref, state_ref, src_index, dst_index,
    qt_ref, at_ref, rel_out, count_ref, column_ref, next_count_ref,
    src_out, state_out, src_index_out, hot0_ref, hot1_ref, picked_ref, meta_ref,
):
    depth, edges = rel_out.shape
    src_out[...] = src_ref[...]
    state_out[...] = state_ref[...]
    src_index_out[...] = src_index[...]
    hot0_ref[...] = one_hot(edges, src_index[0:1, :])
    hot1 = one_hot(edges, src_index[1:2, :])
    hot1_ref[...] = hot1
    picked_ref[...] = picked(src_ref[...], hot1)
    blocks = rows // LANES
    flip = core() * (rows // 2)
    coarse, fine = count_grid(neg_index[0:1, :] ^ flip, blocks)
    lane_row(dot_nt(coarse, fine), count_ref)
    column_ref[...] = dot_nt(fine, coarse)
    coarse, fine = count_grid(neg_index[1:2, :] ^ flip, blocks)
    counts = dot_nt(coarse, fine)
    high = jnp.floor(counts * (1.0 / FINE))
    parts = jnp.concatenate([high, counts - high * FINE], axis=1)
    gap = jnp.zeros((META // 2, edges), F32)
    meta = index_rows(dst_index[1:2, :]).astype(F32)
    meta_ref[...] = (meta + jnp.concatenate([gap, parts], axis=0)).astype(BF)
    lane_row(counts, next_count_ref)
    rel_out[...] = relation_rows(rel_ref, rel_index[1:2, :]).astype(BF)
    query_t, target_at = turned_query(q_ref, depth, flip)
    qt_ref[...] = query_t
    at_ref[...] = jnp.broadcast_to(target_at, at_ref.shape)


def turned_query(q_ref, depth, flip):
    turn = eye(q_ref.shape[1])
    parts = dot_nt(turn, q_ref[depth:, :])
    target_at = (parts[:, 0:1] * FINE + parts[:, 1:2]).astype(I32) ^ flip
    return dot_nt(turn, q_ref[:depth, :]).astype(BF), target_at


def query_gradient(negatives, blocks, query_t, target_at, count_ref):
    total = 0.0
    start = 0
    for block in blocks:
        rows = block.shape[1]
        scores = dot(query_t, block)
        target = iota(scores.shape, 1) + start == target_at
        count = count_ref[:, start : start + rows]
        total += dot_nt(block, coefficients(scores, count, target, negatives))
        start += rows
    return total


def src0_first_kernel(negatives, own_ref, qt_ref, at_ref, count_ref, grad_out):
    half = own_ref.shape[1]
    grad_out[...] = query_gradient(
        negatives, [own_ref[...]], qt_ref[...], at_ref[:, 0:1], count_ref[:, :half]
    )


def src0_kernel(
    negatives, first_ref, other_a, other_b, qt_ref, at_ref, count_ref, src_ref, state_ref,
    rel0_ref, rel1_ref, hot0_ref, hot1_ref, picked_ref, meta_ref, q_ref, src_out, state_out,
):
    depth, edges = src_ref.shape
    block = jnp.concatenate([other_a[...], other_b[...]], axis=1)
    half = block.shape[1]
    grad = first_ref[...] + query_gradient(
        negatives, [block], qt_ref[...], at_ref[:, 0:1] - half, count_ref[:, half:]
    )
    gradient = dot_nt((grad * rel0_ref[...].astype(F32)).astype(BF), hot0_ref[...])
    state, size = step_size(state_ref[...], gradient)
    delta = gradient * size
    src_out[...] = src_ref[...] - delta
    state_out[...] = state
    rows = picked_ref[...] - dot(delta.astype(BF), hot1_ref[...])
    q_ref[:depth, :] = (rows * rel1_ref[...].astype(F32)).astype(BF)
    q_ref[depth:, :] = meta_ref[...]


def src1_kernel(
    negatives, own_ref, other_a, other_b, other_c, q_ref, count_ref, src_ref, state_ref, rel_ref,
    src_index, src_out,
):
    depth, edges = src_ref.shape
    half = own_ref.shape[1]
    query_t, target_at = turned_query(q_ref, depth, core() * half)
    blocks = own_ref[...], jnp.concatenate([other_a[...], other_b[...], other_c[...]], axis=0)
    grad = query_gradient(negatives, blocks, query_t, target_at, count_ref)
    gradient = summed(grad * rel_ref[...].astype(F32), one_hot(edges, src_index[1:2, :]))
    _, size = step_size(state_ref[...], gradient)
    src_out[...] = src_ref[...] - gradient * size


def targets(q_ref, depth, flip):
    parts = q_ref[depth:, :].astype(F32)
    return (parts[0:1, :] * FINE + parts[1:2, :]).astype(I32) ^ flip


def sent_counts(q_ref, depth):
    parts = dot_nt(eye(LANES), q_ref[depth:, :LANES]) * FINE
    parts = parts + dot_nt(eye(LANES), q_ref[depth:, LANES : 2 * LANES])
    return parts[:, META // 2 :]


def row_coefficients(block_t, start, q_ref, column, flip, negatives):
    rows, depth = block_t.shape
    scores = dot(block_t, q_ref[:depth, :])
    target = iota(scores.shape, 0) + start == targets(q_ref, depth, flip)
    first = start // LANES
    count = jnp.concatenate(
        [column[:, first + i : first + i + 1] for i in range(rows // LANES)], axis=0
    )
    return coefficients(scores, count, target, negatives)


def dst_gradient(block_t, q_refs, column, flip, negatives, start=0):
    rows, depth = block_t.shape
    total = jnp.zeros((depth, rows), F32)
    for q_ref in q_refs:
        weights = row_coefficients(block_t, start, q_ref, column, flip, negatives)
        total += dot_nt(q_ref[:depth, :], weights)
    return total


def turned(block):
    step = 2 * LANES
    turn = eye(step)
    return jnp.concatenate(
        [dot_nt(turn, block[:, k : k + step]).astype(BF) for k in range(0, block.shape[1], step)],
        axis=0,
    )


def dst0_kernel(
    negatives, own_ref, old_ref, qa, qb, qc, qd, column_ref,
    block_out, turned_out, delta_out, state_out,
):
    depth, half = delta_out.shape
    block = own_ref[...]
    columns = pl.ds(pl.multiple_of(core() * half, half), half)
    queries = qa, qb, qc, qd
    gradient = dst_gradient(
        turned(block), queries, column_ref[...], core() * half, negatives
    )
    state, size = step_size(old_ref[:, columns], gradient)
    delta = gradient * size
    block = (block.astype(F32) - delta).astype(BF)
    block_out[...] = block
    turned_out[...] = turned(block)
    delta_out[...] = delta
    state_out[...] = state


def dst1_first_kernel(negatives, turned_ref, qa, qb, qc, grad_out, column_out):
    depth, size = grad_out.shape
    column = sent_counts(qa, depth)
    column_out[...] = column
    flip = core() * turned_ref.shape[0]
    grad_out[...] = dst_gradient(turned_ref[:size, :], (qa, qb, qc), column, flip, negatives)


def dst1_kernel(negatives, start, count, turned_ref, column_ref, delta_ref, state_ref, *refs):
    delta_out = refs[-1]
    half = delta_ref.shape[1]
    part = slice(start, start + delta_out.shape[1])
    gradient = dst_gradient(
        turned_ref[part, :], refs[:count], column_ref[...], core() * half, negatives, start
    )
    if start == 0:
        gradient = gradient + refs[count][...]
    _, size = step_size(state_ref[:, part], gradient)
    delta_out[...] = (delta_ref[:, part] + gradient * size).astype(BF)


def final_kernel(start, sides, emb_ref, *refs):
    out_ref, held, sems = refs[-3:]
    half = emb_ref.shape[1] // 2
    copies = []
    for i, (side, count) in enumerate(sides):
        delta = jnp.concatenate([ref[...] for ref in refs[:count]], axis=1)
        refs = refs[count:]
        size = delta.shape[1]
        place = core() if side == 0 else 1 - core()
        columns = pl.ds(pl.multiple_of(place * half + start, size), size)
        held[i] = emb_ref[:, columns] - delta.astype(F32)
        copies.append(pltpu.make_async_copy(held.at[i], out_ref.at[:, columns], sems.at[i]))
        copies[-1].start()
    for copy in copies:
        copy.wait()


def call(kernel, outs, args, name, flops=None, scratch=(), hbm=(), limit=32, out=None):
    vmem = pl.BlockSpec(memory_space=pltpu.VMEM)
    anywhere = pl.BlockSpec(memory_space=pltpu.HBM)
    shapes = [jax.ShapeDtypeStruct(shape, dtype) for shape, dtype in outs]
    size = sum(a.size * a.dtype.itemsize for a in [*args, *shapes])
    result = pl.pallas_call(
        kernel,
        out_shape=shapes,
        in_specs=[anywhere if i in hbm else vmem for i in range(len(args))],
        out_specs=[vmem if out is None else anywhere] * len(shapes),
        input_output_aliases={out: 0} if out else {},
        scratch_shapes=list(scratch),
        compiler_params=pltpu.CompilerParams(vmem_limit_bytes=int(limit * 2**20)),
        cost_estimate=pl.CostEstimate(
            flops=flops or 1, bytes_accessed=size if flops else 1, transcendentals=0
        ),
        name=name,
    )(*args)
    return result[0] if len(shapes) == 1 else result


def body(
    src_emb, src_state, dst_emb, dst_state, relations, src_index, dst_index, rel_index, neg_index
):
    wide, narrow = lax.axis_size("wide"), lax.axis_size("narrow")

    def moved(value, along=0, to=0, copies=False):
        pairs = []
        for w in range(wide):
            target = (w + along) % wide
            other_half = copies and w // (wide // 2) != target // (wide // 2)
            turn = to ^ 2 if other_half else to
            pairs += [(w * narrow + n, target * narrow + (n ^ turn)) for n in range(narrow)]
        return lax.ppermute(value, ("wide", "narrow"), pairs)

    rows, depth = dst_emb.shape
    edges = src_emb.shape[0]
    half = rows // 2
    src_index, dst_index, rel_index, neg_index = (
        a[0] for a in (src_index, dst_index, rel_index, neg_index)
    )
    negatives = neg_index.shape[1]
    dst, src, rel = dst_emb.T, src_emb.T, relations.T
    tall = depth + META

    here = lax.rem(lax.axis_index("narrow"), 2)
    payload = lax.dynamic_slice(dst, (0, here * half), (depth, half)).astype(BF)
    own = moved(payload, along=1, copies=True)
    edges_index = jnp.concatenate([src_index, dst_index, rel_index], axis=0)
    edges_index, payload = lax.optimization_barrier((edges_index, payload))

    src_state = src_state.reshape(1, edges)
    blocks = rows // LANES
    matmul = 2 * edges * rows * depth
    table = 2 * edges * relations.shape[0] * depth
    query, rel0 = call(
        query0_kernel,
        [((tall, edges), BF), ((depth, edges), BF)],
        [rel, src, edges_index],
        "query_step0",
        flops=table,
        limit=32,
    )
    query_c, query_y = moved(query, to=1), moved(query, to=2)
    query, dst_state = lax.optimization_barrier((query, dst_state))
    state = moved(dst_state.reshape(1, rows), along=1, copies=True)
    (
        query_t, target_at, rel1, count0, column, count1,
        src, src_state, src_index, hot0, hot1, picked1, meta1,
    ) = call(
        functools.partial(prep_kernel, rows),
        [
            ((edges, depth), BF),
            ((edges, LANES), I32),
            ((depth, edges), BF),
            ((1, rows), F32),
            ((LANES, blocks), F32),
            ((1, rows), F32),
            (src.shape, F32),
            (src_state.shape, F32),
            (src_index.shape, I32),
            ((edges, edges), BF),
            ((edges, edges), BF),
            (src.shape, F32),
            ((META, edges), BF),
        ],
        [rel, query, rel_index, neg_index, src, src_state, src_index, dst_index],
        "prepare",
        flops=table,
        limit=32,
    )
    own, query_c, rel1, state = lax.optimization_barrier((own, query_c, rel1, state))
    other = [moved(own[:, k : k + half // 2], to=1) for k in (0, half // 2)]

    first = call(
        functools.partial(src0_first_kernel, negatives),
        [((depth, edges), F32)],
        [own, query_t, target_at, count0],
        "source_step0_first",
        limit=24,
    )
    query1, src1, src_state1 = call(
        functools.partial(src0_kernel, negatives),
        [((tall, edges), BF), ((depth, edges), F32), ((1, edges), F32)],
        [
            first, *other, query_t, target_at, count0, src, src_state,
            rel0, rel1, hot0, hot1, picked1, meta1,
        ],
        "source_step0",
        limit=24,
    )
    next_own, next_y = moved(query1, along=-1), moved(query1, along=-1, to=2)
    query_y, query1 = lax.optimization_barrier((query_y, query1))
    query_cy = moved(query_y, to=1)

    block1, turned1, delta0, dst_state1 = call(
        functools.partial(dst0_kernel, negatives),
        [((depth, half), BF), ((half, depth), BF), ((depth, half), F32), ((1, half), F32)],
        [own, state, query, query_y, query_c, query_cy, column],
        "destination_step0",
        limit=24,
    )
    block1_own = moved(block1, along=1, copies=True)
    next_c = moved(next_own, to=1)

    piece = half // 2
    first, column1 = call(
        functools.partial(dst1_first_kernel, negatives),
        [((depth, piece), F32), ((LANES, rows // LANES), F32)],
        [turned1, next_own, next_c, next_y],
        "destination_step1_first",
        limit=24,
    )
    next_cy = moved(next_y, to=1)
    deltas = []
    for start, queries in ((0, [next_cy]), (piece, [next_own, next_c, next_y, next_cy])):
        more = [first] if start == 0 else deltas
        deltas.append(
            call(
                functools.partial(dst1_kernel, negatives, start, len(queries)),
                [((depth, piece), BF)],
                [turned1, column1, delta0, dst_state1, *queries, *more],
                "destination_step1",
                limit=24,
            )
        )
    homes = [moved(delta, along=-1, copies=True) for delta in deltas]

    block1_own, *_ = lax.optimization_barrier((block1_own, *deltas))
    block1_other = [
        moved(block1_own[a:b], to=1) for a, b in zip(ROW_CUTS, (*ROW_CUTS[1:], depth))
    ]
    src_out = call(
        functools.partial(src1_kernel, negatives),
        [((depth, edges), F32)],
        [block1_own, *block1_other, query1, count1, src1, src_state1, rel1, src_index],
        "source_step1",
        limit=24,
    )
    homes[0], src_out = lax.optimization_barrier((homes[0], src_out))
    def final(start, sides, changes, done):
        return call(
            functools.partial(final_kernel, start, sides),
            [((depth, rows), F32)],
            [dst, *changes, *done],
            "destination_out",
            scratch=[
                pltpu.VMEM((len(sides), depth, piece), F32),
                pltpu.SemaphoreType.DMA((len(sides),)),
            ],
            hbm=(1 + len(changes),),
            limit=16,
            out=1 + len(changes) if done else 0,
        )

    cuts = range(0, piece, LANES)
    other = [moved(homes[0][:, k : k + LANES], to=1) for k in cuts]
    dst_out = final(0, ((0, 1), (1, len(other))), [homes[0], *other], ())
    home, dst_out = lax.optimization_barrier((homes[1], dst_out))
    other = moved(home, to=1)
    dst_out = final(piece, ((0, 1),), [home], (dst_out,))
    dst_out = final(piece, ((1, 1),), [other], (dst_out,))
    return src_out.T, dst_out.T


def solution(mesh):
    in_specs = (
        P(("wide", "narrow"), None),
        P(("wide", "narrow")),
        P("wide", None),
        P("wide"),
        P(),
        P(("wide", "narrow"), None, None),
        P(("wide", "narrow"), None, None),
        P(("wide", "narrow"), None, None),
        P("wide", None, None),
    )
    out_specs = (P(("wide", "narrow"), None), P("wide", None))
    return jax.shard_map(body, mesh=mesh, in_specs=in_specs, out_specs=out_specs, check_vma=False)
```

```python
import functools

import jax
import jax.numpy as jnp
from jax import lax
from jax.experimental import pallas as pl
from jax.experimental.pallas import tpu as pltpu
from jax.sharding import PartitionSpec as P

LEARNING_RATE = 0.1
BF = jnp.bfloat16
F32 = jnp.float32
I32 = jnp.int32
META = 16
FINE = 32
LANES = 128
ROW_CUTS = 0, 144, 272
PIECE = 1920


def dot(a, b):
    return lax.dot_general(a, b, (((1,), (0,)), ((), ())), preferred_element_type=F32)


def dot_nt(a, b):
    return lax.dot_general(a, b, (((1,), (1,)), ((), ())), preferred_element_type=F32)


def core():
    return lax.rem(lax.axis_index("narrow"), 2)


def iota(shape, dim):
    return lax.broadcasted_iota(I32, shape, dim)


def one_hot(rows, index):
    return (iota((rows, index.shape[1]), 0) == index).astype(F32).astype(BF)


def eye(n):
    return (iota((n, n), 0) == iota((n, n), 1)).astype(F32).astype(BF)


def index_rows(index):
    fine = lax.rem(index, FINE)
    coarse = lax.div(index, FINE)
    at = iota((META, index.shape[1]), 0)
    parts = jnp.where(at == 0, coarse, jnp.where(at == 1, fine, 0))
    return parts.astype(F32).astype(BF)


def split(value):
    high = value.astype(BF)
    return high, (value - high.astype(F32)).astype(BF)


def picked(value, hot):
    high, low = split(value)
    return dot(high, hot) + dot(low, hot)


def summed(value, hot):
    high, low = split(value)
    return dot_nt(high, hot) + dot_nt(low, hot)


def coefficients(scores, count, is_target, negatives):
    tanh = jnp.tanh(0.5 * scores)
    scale = count * (0.5 / negatives)
    pull = jnp.where(is_target, 0.5 * tanh - 0.5, 0.0)
    return (scale * tanh + scale + pull).astype(BF)


def step_size(state, gradient):
    state = state + jnp.mean(gradient * gradient, axis=0, keepdims=True)
    return state, LEARNING_RATE / jnp.sqrt(state)


def count_grid(index, blocks):
    return one_hot(blocks, lax.div(index, LANES)), one_hot(LANES, lax.rem(index, LANES))


def relation_rows(rel_ref, index):
    depth, relations = rel_ref.shape
    block = lax.div(index, LANES)
    within = one_hot(LANES, lax.rem(index, LANES))
    found = jnp.zeros((depth, index.shape[1]), F32)
    for start in range(0, relations, PIECE):
        size = min(PIECE, relations - start)
        hot = jnp.concatenate(
            [
                within * (block == start // LANES + i).astype(F32).astype(BF)
                for i in range(size // LANES)
            ],
            axis=0,
        )
        found = found + dot(rel_ref[:, start : start + size], hot)
    return found


def lane_row(counts, out_ref):
    for i in range(counts.shape[0]):
        out_ref[:, i * LANES : (i + 1) * LANES] = counts[i : i + 1, :]


def query0_kernel(
    rel_ref, src_ref, index, q_ref, rel_out
):
    depth, edges = src_ref.shape
    src_index, dst_index, rel_index = index[0:1, :], index[2:3, :], index[4:5, :]
    found = relation_rows(rel_ref, rel_index)
    rel_out[...] = found.astype(BF)
    rows = picked(src_ref[...], one_hot(edges, src_index))
    q_ref[:depth, :] = (rows * found).astype(BF)
    q_ref[depth:, :] = index_rows(dst_index)


def prep_kernel(
    rows, rel_ref, q_ref, rel_index, neg_index, src_ref, state_ref, src_index, dst_index,
    qt_ref, at_ref, rel_out, count_ref, column_ref, next_count_ref,
    src_out, state_out, src_index_out, hot0_ref, hot1_ref, picked_ref, meta_ref,
):
    depth, edges = rel_out.shape
    src_out[...] = src_ref[...]
    state_out[...] = state_ref[...]
    src_index_out[...] = src_index[...]
    hot0_ref[...] = one_hot(edges, src_index[0:1, :])
    hot1 = one_hot(edges, src_index[1:2, :])
    hot1_ref[...] = hot1
    picked_ref[...] = picked(src_ref[...], hot1)
    blocks = rows // LANES
    flip = core() * (rows // 2)
    coarse, fine = count_grid(neg_index[0:1, :] ^ flip, blocks)
    lane_row(dot_nt(coarse, fine), count_ref)
    column_ref[...] = dot_nt(fine, coarse)
    coarse, fine = count_grid(neg_index[1:2, :] ^ flip, blocks)
    counts = dot_nt(coarse, fine)
    high = jnp.floor(counts * (1.0 / FINE))
    parts = jnp.concatenate([high, counts - high * FINE], axis=1)
    gap = jnp.zeros((META // 2, edges), F32)
    meta = index_rows(dst_index[1:2, :]).astype(F32)
    meta_ref[...] = (meta + jnp.concatenate([gap, parts], axis=0)).astype(BF)
    lane_row(counts, next_count_ref)
    rel_out[...] = relation_rows(rel_ref, rel_index[1:2, :]).astype(BF)
    query_t, target_at = turned_query(q_ref, depth, flip)
    qt_ref[...] = query_t
    at_ref[...] = jnp.broadcast_to(target_at, at_ref.shape)


def turned_query(q_ref, depth, flip):
    turn = eye(q_ref.shape[1])
    parts = dot_nt(turn, q_ref[depth:, :])
    target_at = (parts[:, 0:1] * FINE + parts[:, 1:2]).astype(I32) ^ flip
    return dot_nt(turn, q_ref[:depth, :]).astype(BF), target_at


def query_gradient(negatives, blocks, query_t, target_at, count_ref):
    total = 0.0
    start = 0
    for block in blocks:
        rows = block.shape[1]
        scores = dot(query_t, block)
        target = iota(scores.shape, 1) + start == target_at
        count = count_ref[:, start : start + rows]
        total += dot_nt(block, coefficients(scores, count, target, negatives))
        start += rows
    return total


def src0_first_kernel(negatives, own_ref, qt_ref, at_ref, count_ref, grad_out):
    half = own_ref.shape[1]
    grad_out[...] = query_gradient(
        negatives, [own_ref[...]], qt_ref[...], at_ref[:, 0:1], count_ref[:, :half]
    )


def src0_kernel(
    negatives, first_ref, other_a, other_b, qt_ref, at_ref, count_ref, src_ref, state_ref,
    rel0_ref, rel1_ref, hot0_ref, hot1_ref, picked_ref, meta_ref, q_ref, src_out, state_out,
):
    depth, edges = src_ref.shape
    block = jnp.concatenate([other_a[...], other_b[...]], axis=1)
    half = block.shape[1]
    grad = first_ref[...] + query_gradient(
        negatives, [block], qt_ref[...], at_ref[:, 0:1] - half, count_ref[:, half:]
    )
    gradient = dot_nt((grad * rel0_ref[...].astype(F32)).astype(BF), hot0_ref[...])
    state, size = step_size(state_ref[...], gradient)
    delta = gradient * size
    src_out[...] = src_ref[...] - delta
    state_out[...] = state
    rows = picked_ref[...] - dot(delta.astype(BF), hot1_ref[...])
    q_ref[:depth, :] = (rows * rel1_ref[...].astype(F32)).astype(BF)
    q_ref[depth:, :] = meta_ref[...]


def src1_kernel(
    negatives, own_ref, other_a, other_b, other_c, q_ref, count_ref, src_ref, state_ref, rel_ref,
    src_index, src_out,
):
    depth, edges = src_ref.shape
    half = own_ref.shape[1]
    query_t, target_at = turned_query(q_ref, depth, core() * half)
    blocks = own_ref[...], jnp.concatenate([other_a[...], other_b[...], other_c[...]], axis=0)
    grad = query_gradient(negatives, blocks, query_t, target_at, count_ref)
    gradient = summed(grad * rel_ref[...].astype(F32), one_hot(edges, src_index[1:2, :]))
    _, size = step_size(state_ref[...], gradient)
    src_out[...] = src_ref[...] - gradient * size


def targets(q_ref, depth, flip):
    parts = q_ref[depth:, :].astype(F32)
    return (parts[0:1, :] * FINE + parts[1:2, :]).astype(I32) ^ flip


def sent_counts(q_ref, depth):
    parts = dot_nt(eye(LANES), q_ref[depth:, :LANES]) * FINE
    parts = parts + dot_nt(eye(LANES), q_ref[depth:, LANES : 2 * LANES])
    return parts[:, META // 2 :]


def row_coefficients(block_t, start, q_ref, column, flip, negatives):
    rows, depth = block_t.shape
    scores = dot(block_t, q_ref[:depth, :])
    target = iota(scores.shape, 0) + start == targets(q_ref, depth, flip)
    first = start // LANES
    count = jnp.concatenate(
        [column[:, first + i : first + i + 1] for i in range(rows // LANES)], axis=0
    )
    return coefficients(scores, count, target, negatives)


def dst_gradient(block_t, q_refs, column, flip, negatives, start=0):
    rows, depth = block_t.shape
    total = jnp.zeros((depth, rows), F32)
    for q_ref in q_refs:
        weights = row_coefficients(block_t, start, q_ref, column, flip, negatives)
        total += dot_nt(q_ref[:depth, :], weights)
    return total


def turned(block):
    step = 2 * LANES
    turn = eye(step)
    return jnp.concatenate(
        [dot_nt(turn, block[:, k : k + step]).astype(BF) for k in range(0, block.shape[1], step)],
        axis=0,
    )


def dst0_kernel(
    negatives, own_ref, old_ref, qa, qb, qc, qd, column_ref,
    block_out, turned_out, delta_out, state_out,
):
    depth, half = delta_out.shape
    block = own_ref[...]
    columns = pl.ds(pl.multiple_of(core() * half, half), half)
    queries = qa, qb, qc, qd
    gradient = dst_gradient(
        turned(block), queries, column_ref[...], core() * half, negatives
    )
    state, size = step_size(old_ref[:, columns], gradient)
    delta = gradient * size
    block = (block.astype(F32) - delta).astype(BF)
    block_out[...] = block
    turned_out[...] = turned(block)
    delta_out[...] = delta
    state_out[...] = state


def dst1_first_kernel(negatives, turned_ref, qa, qb, qc, grad_out, column_out):
    depth, size = grad_out.shape
    column = sent_counts(qa, depth)
    column_out[...] = column
    flip = core() * turned_ref.shape[0]
    grad_out[...] = dst_gradient(turned_ref[:size, :], (qa, qb, qc), column, flip, negatives)


def dst1_kernel(negatives, start, count, turned_ref, column_ref, delta_ref, state_ref, *refs):
    delta_out = refs[-1]
    half = delta_ref.shape[1]
    part = slice(start, start + delta_out.shape[1])
    gradient = dst_gradient(
        turned_ref[part, :], refs[:count], column_ref[...], core() * half, negatives, start
    )
    if start == 0:
        gradient = gradient + refs[count][...]
    _, size = step_size(state_ref[:, part], gradient)
    delta_out[...] = (delta_ref[:, part] + gradient * size).astype(BF)


def final_kernel(start, sides, emb_ref, *refs):
    out_ref, held, sems = refs[-3:]
    half = emb_ref.shape[1] // 2
    copies = []
    for i, (side, count) in enumerate(sides):
        delta = jnp.concatenate([ref[...] for ref in refs[:count]], axis=1)
        refs = refs[count:]
        size = delta.shape[1]
        place = core() if side == 0 else 1 - core()
        columns = pl.ds(pl.multiple_of(place * half + start, size), size)
        held[i] = emb_ref[:, columns] - delta.astype(F32)
        copies.append(pltpu.make_async_copy(held.at[i], out_ref.at[:, columns], sems.at[i]))
        copies[-1].start()
    for copy in copies:
        copy.wait()


def call(kernel, outs, args, name, flops=None, scratch=(), hbm=(), limit=32, out=None):
    vmem = pl.BlockSpec(memory_space=pltpu.VMEM)
    anywhere = pl.BlockSpec(memory_space=pltpu.HBM)
    shapes = [jax.ShapeDtypeStruct(shape, dtype) for shape, dtype in outs]
    size = sum(a.size * a.dtype.itemsize for a in [*args, *shapes])
    result = pl.pallas_call(
        kernel,
        out_shape=shapes,
        in_specs=[anywhere if i in hbm else vmem for i in range(len(args))],
        out_specs=[vmem if out is None else anywhere] * len(shapes),
        input_output_aliases={out: 0} if out else {},
        scratch_shapes=list(scratch),
        compiler_params=pltpu.CompilerParams(vmem_limit_bytes=int(limit * 2**20)),
        cost_estimate=pl.CostEstimate(
            flops=flops or 1, bytes_accessed=size if flops else 1, transcendentals=0
        ),
        name=name,
    )(*args)
    return result[0] if len(shapes) == 1 else result


def body(
    src_emb, src_state, dst_emb, dst_state, relations, src_index, dst_index, rel_index, neg_index
):
    wide, narrow = lax.axis_size("wide"), lax.axis_size("narrow")

    def moved(value, along=0, to=0, copies=False):
        pairs = []
        for w in range(wide):
            target = (w + along) % wide
            other_half = copies and w // (wide // 2) != target // (wide // 2)
            turn = to ^ 2 if other_half else to
            pairs += [(w * narrow + n, target * narrow + (n ^ turn)) for n in range(narrow)]
        return lax.ppermute(value, ("wide", "narrow"), pairs)

    rows, depth = dst_emb.shape
    edges = src_emb.shape[0]
    half = rows // 2
    src_index, dst_index, rel_index, neg_index = (
        a[0] for a in (src_index, dst_index, rel_index, neg_index)
    )
    negatives = neg_index.shape[1]
    dst, src, rel = dst_emb.T, src_emb.T, relations.T
    tall = depth + META

    here = lax.rem(lax.axis_index("narrow"), 2)
    payload = lax.dynamic_slice(dst, (0, here * half), (depth, half)).astype(BF)
    own = moved(payload, along=1, copies=True)
    edges_index = jnp.concatenate([src_index, dst_index, rel_index], axis=0)
    edges_index, payload = lax.optimization_barrier((edges_index, payload))

    src_state = src_state.reshape(1, edges)
    blocks = rows // LANES
    matmul = 2 * edges * rows * depth
    table = 2 * edges * relations.shape[0] * depth
    query, rel0 = call(
        query0_kernel,
        [((tall, edges), BF), ((depth, edges), BF)],
        [rel, src, edges_index],
        "query_step0",
        flops=table,
        limit=32,
    )
    query_c, query_y = moved(query, to=1), moved(query, to=2)
    query, dst_state = lax.optimization_barrier((query, dst_state))
    state = moved(dst_state.reshape(1, rows), along=1, copies=True)
    (
        query_t, target_at, rel1, count0, column, count1,
        src, src_state, src_index, hot0, hot1, picked1, meta1,
    ) = call(
        functools.partial(prep_kernel, rows),
        [
            ((edges, depth), BF),
            ((edges, LANES), I32),
            ((depth, edges), BF),
            ((1, rows), F32),
            ((LANES, blocks), F32),
            ((1, rows), F32),
            (src.shape, F32),
            (src_state.shape, F32),
            (src_index.shape, I32),
            ((edges, edges), BF),
            ((edges, edges), BF),
            (src.shape, F32),
            ((META, edges), BF),
        ],
        [rel, query, rel_index, neg_index, src, src_state, src_index, dst_index],
        "prepare",
        flops=table,
        limit=32,
    )
    own, query_c, rel1, state = lax.optimization_barrier((own, query_c, rel1, state))
    other = [moved(own[:, k : k + half // 2], to=1) for k in (0, half // 2)]

    first = call(
        functools.partial(src0_first_kernel, negatives),
        [((depth, edges), F32)],
        [own, query_t, target_at, count0],
        "source_step0_first",
        limit=24,
    )
    query1, src1, src_state1 = call(
        functools.partial(src0_kernel, negatives),
        [((tall, edges), BF), ((depth, edges), F32), ((1, edges), F32)],
        [
            first, *other, query_t, target_at, count0, src, src_state,
            rel0, rel1, hot0, hot1, picked1, meta1,
        ],
        "source_step0",
        limit=24,
    )
    next_own, next_y = (moved(query1, along=-1, to=to, copies=True) for to in (0, 2))
    query_y, query1 = lax.optimization_barrier((query_y, query1))
    query_cy = moved(query_y, to=1)

    block1, turned1, delta0, dst_state1 = call(
        functools.partial(dst0_kernel, negatives),
        [((depth, half), BF), ((half, depth), BF), ((depth, half), F32), ((1, half), F32)],
        [own, state, query, query_y, query_c, query_cy, column],
        "destination_step0",
        limit=24,
    )
    block1_own = moved(block1, along=1, copies=True)
    next_c = moved(next_own, to=1)

    piece = half // 2
    first, column1 = call(
        functools.partial(dst1_first_kernel, negatives),
        [((depth, piece), F32), ((LANES, rows // LANES), F32)],
        [turned1, next_own, next_c, next_y],
        "destination_step1_first",
        limit=24,
    )
    next_cy = moved(next_y, to=1)
    deltas = []
    for start, queries in ((0, [next_cy]), (piece, [next_own, next_c, next_y, next_cy])):
        more = [first] if start == 0 else deltas
        deltas.append(
            call(
                functools.partial(dst1_kernel, negatives, start, len(queries)),
                [((depth, piece), BF)],
                [turned1, column1, delta0, dst_state1, *queries, *more],
                "destination_step1",
                limit=24,
            )
        )
    homes = [moved(delta, along=-1, copies=True) for delta in deltas]

    block1_own, *_ = lax.optimization_barrier((block1_own, *deltas))
    block1_other = [
        moved(block1_own[a:b], to=1) for a, b in zip(ROW_CUTS, (*ROW_CUTS[1:], depth))
    ]
    src_out = call(
        functools.partial(src1_kernel, negatives),
        [((depth, edges), F32)],
        [block1_own, *block1_other, query1, count1, src1, src_state1, rel1, src_index],
        "source_step1",
        limit=24,
    )
    homes[0], src_out = lax.optimization_barrier((homes[0], src_out))
    def final(start, sides, changes, done):
        return call(
            functools.partial(final_kernel, start, sides),
            [((depth, rows), F32)],
            [dst, *changes, *done],
            "destination_out",
            scratch=[
                pltpu.VMEM((len(sides), depth, piece), F32),
                pltpu.SemaphoreType.DMA((len(sides),)),
            ],
            hbm=(1 + len(changes),),
            limit=16,
            out=1 + len(changes) if done else 0,
        )

    cuts = range(0, piece, LANES)
    other = [moved(homes[0][:, k : k + LANES], to=1) for k in cuts]
    dst_out = final(0, ((0, 1), (1, len(other))), [homes[0], *other], ())
    home, dst_out = lax.optimization_barrier((homes[1], dst_out))
    other = moved(home, to=1)
    dst_out = final(piece, ((0, 1),), [home], (dst_out,))
    dst_out = final(piece, ((1, 1),), [other], (dst_out,))
    return src_out.T, dst_out.T


def solution(mesh):
    in_specs = (
        P(("wide", "narrow"), None),
        P(("wide", "narrow")),
        P("wide", None),
        P("wide"),
        P(),
        P(("wide", "narrow"), None, None),
        P(("wide", "narrow"), None, None),
        P(("wide", "narrow"), None, None),
        P("wide", None, None),
    )
    out_specs = (P(("wide", "narrow"), None), P("wide", None))
    return jax.shard_map(body, mesh=mesh, in_specs=in_specs, out_specs=out_specs, check_vma=False)
```
